32 devices in a mesh: fsdp: 8 (over z, y), rep: 4 (over x, core).
Axes of the slice: x: 2, y: 2, z: 4, core: 2. Of those that a mesh axis runs over, the one named last changes fastest.
Arguments:
- tokens: bfloat16 [32768, 768], P(('fsdp', 'rep')), may hold values from -6 to 6
- lengths: int32 [32, 2], P(('fsdp', 'rep')), may hold values from 0 to 1024, as said below
- w_qkv: bfloat16 [768, 2304], P('fsdp'), may hold values from -0.21875 to 0.21875
- vectors: bfloat16 [8, 768], P(None, 'fsdp')
- w_attn_out: bfloat16 [768, 768], P('fsdp'), may hold values from -2 to 2
- w_in: bfloat16 [768, 3072], P('fsdp'), may hold values from -0.21875 to 0.21875
- b_in: bfloat16 [3072], P('fsdp'), may hold values from -3 to 3
- w_down: bfloat16 [3072, 768], P('fsdp'), may hold values from -0.109375 to 0.109375
- cotangent: bfloat16 [32768, 768], P(('fsdp', 'rep')), may hold values from -6 to 6
Outputs:
- layer_out: bfloat16 [32768, 768], P(('fsdp', 'rep'))
- grad_tokens: bfloat16 [32768, 768], P(('fsdp', 'rep'))
- grad_w_qkv: float32 [768, 2304], P('fsdp')
- grad_vectors: float32 [8, 768], P(None, 'fsdp')
- grad_w_attn_out: float32 [768, 768], P('fsdp')
- grad_w_in: float32 [768, 3072], P('fsdp')
- grad_b_in: float32 [3072], P('fsdp')
- grad_w_down: float32 [3072, 768], P('fsdp')
The draws below stay inside these ranges and needn't reach their ends.
Inputs may be any that keep to these rules, and one draw needn't show every extreme that they name: Row g holds the lengths of the two sequences of the g-th group of 1024 tokens (groups in the order of the token rows). The first starts at the group's row 0, the second at the first multiple of 128 at or after the first one's end, and both end within the group. One group holds a single sequence of 1024 tokens and a second of length 0; every other group has two sequences of 1 or more tokens.
All inputs are finite; a program needn't handle non-finite values.
Results may differ from the reference program's by a relative error of at most 0.017.
Values may be sent and summed in bfloat16 or wider, within the bound.
No kernel may reach another device: no remote copies, remote signals or barrier semaphores. Data moves between devices by JAX's collectives and lax.ppermute only.
A program may use at most 256 MiB of HBM per device.

```python
import jax
import jax.numpy as jnp
from jax import lax

D = 768
HEADS = 12
HEAD_DIM = 64
FF = 3072
BLOCK = 128
BLK_DEV = 8
TOK_DEV = 1024
GROUPS = 32
TOKENS = 32768


def draw_lengths(key, part):
    key = jax.random.fold_in(key, 7)
    keys_used = jax.random.split(key, 5)
    used_blocks = jax.random.randint(keys_used[0], (GROUPS,), BLK_DEV // 2, BLK_DEV + 1)
    first_blocks = jax.random.randint(keys_used[1], (GROUPS,), 1, used_blocks)
    first_len = first_blocks * BLOCK - jax.random.randint(keys_used[2], (GROUPS,), 0, BLOCK)
    second_len = (used_blocks - first_blocks) * BLOCK - jax.random.randint(keys_used[3], (GROUPS,), 0, BLOCK)
    chosen = jax.random.randint(keys_used[4], (), 0, GROUPS)
    is_full = jnp.arange(GROUPS) == chosen
    first_len = jnp.where(is_full, BLK_DEV * BLOCK, first_len)
    second_len = jnp.where(is_full, 0, second_len)
    return jnp.stack([first_len, second_len], axis=1).astype(jnp.int32)


def draw_vectors(key, part):
    key = jax.random.fold_in(key, 3)
    spread = jnp.array([0.5, 0.5, 0.3, 0.15, 0.3, 0.3, 0.15, 0.3], jnp.float32)[:, None]
    centre = jnp.array([0.0, 0.0, 0.0, 1.0, 0.0, 0.0, 1.0, 0.0], jnp.float32)[:, None]
    noise_rows = jnp.clip(jax.random.normal(key, (8, D), jnp.float32), -3.0, 3.0)
    return (centre + spread * noise_rows).astype(jnp.bfloat16)


def block_scale(own_key, extent, cuts, smallest, high):
    def one(axis_at, shards_of):
        steps = jax.random.uniform(jax.random.fold_in(jax.random.fold_in(own_key, 6), axis_at), (shards_of,), jnp.float32, smallest / len(cuts), high / len(cuts))
        return jnp.repeat(jnp.exp(steps), extent[axis_at] // shards_of).reshape((-1,) + (1,) * (len(extent) - axis_at - 1))

    loudness = one(*cuts[0])
    for cut in cuts[1:]:
        loudness = loudness * one(*cut)
    return loudness


def scatter_about(own_key, shape, scale, most, pieces=(), kind=jnp.bfloat16):
    level = block_scale(own_key, shape, pieces, -0.22, 0.18) if pieces else 1.0
    values = jax.random.normal(own_key, shape, jnp.float32) * scale * level
    return jnp.minimum(jnp.maximum(values, -most), most).astype(kind)


def setup_inputs(seed: int = 0) -> dict:
    seeds = jax.random.split(jax.random.key(seed), 10)
    tokens = scatter_about(seeds[0], (TOKENS, D), 1.0, 6.0, ((0, 32),))
    lengths = draw_lengths(jax.random.fold_in(seeds[9], 71), 0)
    w_qkv = scatter_about(seeds[2], (D, 3 * D), D ** -0.5, 0.21875, ((0, 8),))
    vectors = draw_vectors(jax.random.fold_in(seeds[9], 71), 0)
    w_attn_out = scatter_about(seeds[4], (D, D), (max(2, D // 96)) ** -0.5, 2.0, ((0, 8),))
    w_in = scatter_about(seeds[5], (D, FF), D ** -0.5, 0.21875, ((0, 8),))
    b_in = scatter_about(seeds[6], (FF,), 0.5, 3.0, ((0, 8),))
    w_down = scatter_about(seeds[7], (FF, D), FF ** -0.5, 0.109375, ((0, 8),))
    cotangent = scatter_about(seeds[8], (TOKENS, D), 1.0, 6.0, ((0, 32),))
    return dict(tokens=tokens, lengths=lengths, w_qkv=w_qkv, vectors=vectors, w_attn_out=w_attn_out, w_in=w_in, b_in=b_in, w_down=w_down, cotangent=cotangent)


NORM_EPS = 1e-12
MASKED_SCORE = -1e+30
HIGHEST = lax.Precision.HIGHEST

@jax.custom_vjp
def low(v):
    return lax.optimization_barrier(v.astype(jnp.bfloat16)).astype(jnp.float32)

@jax.custom_vjp
def low_back(v):
    return v

def low_keep(v):
    return (low(v), None)

def low_pass(kept, grad):
    return (grad,)

def back_keep(v):
    return (v, None)

def back_low(kept, grad):
    return (low(grad),)
low.defvjp(low_keep, low_pass)
low_back.defvjp(back_keep, back_low)

def layout(length_row, row_count):
    first_len = length_row[0]
    second_len = length_row[1]
    second_start = (first_len + BLOCK - 1) // BLOCK * BLOCK
    positions = jnp.arange(row_count, dtype=jnp.int32)
    in_first = positions < first_len
    in_second = (positions >= second_start) & (positions < second_start + second_len)
    doc_ids = jnp.where(in_first, 0, jnp.where(in_second, 1, 2)).astype(jnp.int32)
    return (in_first | in_second, doc_ids)

def norm_rows(hidden, gain_row, shift_row):
    centre = lax.optimization_barrier(jnp.mean(hidden, axis=-1, keepdims=True))
    spread = lax.optimization_barrier(jnp.mean(jnp.square(hidden - centre), axis=-1, keepdims=True))
    return (hidden - centre) * lax.rsqrt(spread + NORM_EPS) * gain_row + shift_row

def one_group(tok_rows, length_row, w_qkv, vectors, w_attn_out, w_in, b_in, w_down):
    row_count = tok_rows.shape[0]
    valid_rows, doc_ids = layout(length_row, row_count)
    projected = jnp.dot(tok_rows, w_qkv, precision=HIGHEST)
    queries = low_back(low(projected[:, :D] + vectors[0]))
    key_rows = low_back(low(projected[:, D:2 * D]))
    value_rows = low_back(low(projected[:, 2 * D:] + vectors[1]))
    rows_block = min(512, row_count)
    blocks = row_count // rows_block
    key_split = key_rows.reshape(row_count, HEADS, HEAD_DIM)
    value_split = value_rows.reshape(row_count, HEADS, HEAD_DIM)

    def attend(block_pair):
        query_part, doc_part = block_pair
        allowed = doc_part[:, None] == doc_ids[None, :]
        scores = jnp.einsum('qhd,khd->hqk', query_part, key_split, precision=HIGHEST) * 0.125
        scores = jnp.where(allowed[None], low_back(scores), MASKED_SCORE)
        weights = low(jax.nn.softmax(scores, axis=-1))
        return jnp.einsum('hqk,khd->qhd', weights, value_split, precision=HIGHEST)
    attended = lax.map(jax.checkpoint(attend), (queries.reshape(blocks, rows_block, HEADS, HEAD_DIM), doc_ids.reshape(blocks, rows_block)))
    context = low_back(low(attended.reshape(row_count, D)))
    attn_branch = low_back(jnp.dot(context, w_attn_out, precision=HIGHEST) + vectors[2])
    first_norm = norm_rows(tok_rows + attn_branch, vectors[3], vectors[4])
    inner_act = low_back(jnp.dot(low(first_norm), w_in, precision=HIGHEST) + b_in)
    active = low(jax.nn.gelu(inner_act, approximate=False))
    mlp_branch = low_back(jnp.dot(active, w_down, precision=HIGHEST) + vectors[5])
    second_norm = norm_rows(first_norm + mlp_branch, vectors[6], vectors[7])
    return jnp.where(valid_rows[:, None], second_norm, 0.0)

def reference(tokens, lengths, w_qkv, vectors, w_attn_out, w_in, b_in, w_down, cotangent):

    def forward(tok_all, qkv_mat, vector_rows, out_mat, in_mat, in_bias, down_mat):

        def group_step(group_pair):
            return one_group(group_pair[0], group_pair[1], qkv_mat, vector_rows, out_mat, in_mat, in_bias, down_mat)
        grouped = lax.map(jax.checkpoint(group_step), (tok_all.reshape(GROUPS, TOK_DEV, D), lengths))
        return grouped.reshape(TOKENS, D)
    result, pull_back = jax.vjp(forward, tokens.astype(jnp.float32), w_qkv.astype(jnp.float32), vectors.astype(jnp.float32), w_attn_out.astype(jnp.float32), w_in.astype(jnp.float32), b_in.astype(jnp.float32), w_down.astype(jnp.float32))
    grads = pull_back(cotangent.astype(jnp.float32))
    return (result.astype(jnp.bfloat16), grads[0].astype(jnp.bfloat16), grads[1], grads[2], grads[3], grads[4], grads[5], grads[6])
```

```python
import functools
import math

import jax
import jax.numpy as jnp
from jax import lax
from jax.experimental import pallas as pl
from jax.experimental.pallas import tpu as pltpu
from jax.sharding import PartitionSpec as P

D = 768
HEADS = 12
HEAD_DIM = 64
BLOCK = 128

NORM_EPS = 1e-12
MASKED_SCORE = -1e30
SCALE_TWO = 0.125 * math.log2(math.e)
MIB = 1 << 20

NT = (((1,), (1,)), ((), ()))
TN = (((0,), (0,)), ((), ()))


def wide_dot(left, right, dims=(((1,), (0,)), ((), ()))):
    return lax.dot_general(left, right, dims, preferred_element_type=jnp.float32)


def vmem(mib):
    return pltpu.CompilerParams(vmem_limit_bytes=mib * MIB)


def layout(length_row, row_count):
    first_len = length_row[0]
    second_len = length_row[1]
    second_start = (first_len + BLOCK - 1) // BLOCK * BLOCK
    positions = jnp.arange(row_count, dtype=jnp.int32)
    in_first = positions < first_len
    in_second = (positions >= second_start) & (positions < second_start + second_len)
    doc_ids = jnp.where(in_first, 0, jnp.where(in_second, 1, 2)).astype(jnp.int32)
    return (in_first | in_second, doc_ids)


def norm_forward(hidden, gain_row, shift_row):
    centre = jnp.mean(hidden, axis=-1, keepdims=True)
    spread = jnp.mean(jnp.square(hidden - centre), axis=-1, keepdims=True)
    inverse = lax.rsqrt(spread + NORM_EPS)
    normed = (hidden - centre) * inverse
    return (normed * gain_row + shift_row, normed, inverse)


def norm_backward(grad_rows, normed, inverse, gain_row):
    scaled = grad_rows * gain_row
    grad_in = inverse * (
        scaled
        - jnp.mean(scaled, axis=-1, keepdims=True)
        - normed * jnp.mean(scaled * normed, axis=-1, keepdims=True)
    )
    return (grad_in, jnp.sum(grad_rows * normed, axis=0), jnp.sum(grad_rows, axis=0))


LANES = 384
ROWS = 96


class Place:
    def __init__(self):
        fsdp, rep = lax.axis_index("fsdp"), lax.axis_index("rep")
        self.z, self.y = fsdp // 2, fsdp % 2
        self.x, self.c = rep // 2, rep % 2
        self.scalars = jnp.stack([self.z, self.y, self.x, self.c]).astype(jnp.int32)


def swap_core(rows):
    return lax.ppermute(rows, "rep", [(i, i ^ 1) for i in range(4)])


def swap_x(rows):
    return lax.ppermute(rows, "rep", [(i, i ^ 2) for i in range(4)])


def swap_y(rows):
    return lax.ppermute(rows, "fsdp", [(i, i ^ 1) for i in range(8)])


def turn_z(rows, step):
    return lax.ppermute(rows, "fsdp", [(i, (i + 2 * step) % 8) for i in range(8)])


def pick(rows, index):
    return lax.dynamic_index_in_dim(rows, index, 0, keepdims=False)


def after(rows, *others):
    return lax.optimization_barrier((rows, *others))[0]


def gather_z(own):
    return jnp.stack([own] + [turn_z(own, step) for step in (1, 2, 3)])


def place_kernel(split_x, down, nb, near_ref, *refs):
    pieces, full_ref = refs[:-1], refs[-1]
    z, y, x, c = near_ref[0], near_ref[1], near_ref[2], near_ref[3]
    for p, piece in enumerate(pieces):
        far_y, far_x, far_c = (p & 1, (p >> 1) & 1, p >> 2) if split_x else (p & 1, 0, p >> 1)
        core = 1 - c if far_c else c
        side = 1 - x if far_x else x
        for k in range(4):
            f = lax.rem(z + 4 - k, 4) * 2 + (1 - y if far_y else y)
            for j in range(nb):
                inner = side * nb + j if split_x else j
                half = 2 * nb if split_x else nb
                if down:
                    row, col = f * (half * ROWS) + inner * ROWS, core * LANES
                else:
                    row, col = f * ROWS, (core * half + inner) * LANES
                row, col = pl.multiple_of(row, ROWS), pl.multiple_of(col, LANES)
                full_ref[pl.ds(row, ROWS), pl.ds(col, LANES)] = (
                    piece[k, j] if piece.shape[2] == ROWS else piece[k, 0, j * ROWS : (j + 1) * ROWS]
                )


def put_together(near, pieces, nb, shape, split_x, down):
    return pl.pallas_call(
        functools.partial(place_kernel, split_x, down, nb),
        out_shape=jax.ShapeDtypeStruct(shape, jnp.bfloat16),
        in_specs=[pl.BlockSpec(memory_space=pltpu.SMEM)]
        + [pl.BlockSpec(memory_space=pltpu.VMEM)] * len(pieces),
        out_specs=pl.BlockSpec(memory_space=pltpu.VMEM),
        compiler_params=vmem(16),
        cost_estimate=pl.CostEstimate(
            flops=0, bytes_accessed=4 * shape[0] * shape[1], transcendentals=0
        ),
    )(near, *pieces)


def to_blocks(shard, down):
    if down:
        return shard.reshape(4, ROWS, 2, LANES).transpose(2, 0, 1, 3).reshape(8, ROWS, LANES)
    return shard.reshape(ROWS, -1, LANES).transpose(1, 0, 2)


def own_blocks(blocks, place, split_x):
    half = blocks.shape[0] // 2
    if split_x:
        return lax.dynamic_slice_in_dim(
            blocks, place.c * half + place.x * (half // 2), half // 2, 0
        )
    return lax.dynamic_slice_in_dim(blocks, place.c * half, half, 0)


def gather_rest_of(place, pieces, nb, shape, split_x, down):
    if split_x:
        pieces = pieces + [swap_x(piece) for piece in pieces]
    pieces = pieces + [swap_core(piece) for piece in pieces]
    return put_together(place.scalars, pieces, nb, shape, split_x, down)


def gather_rest(place, near, shape, split_x, down):
    return gather_rest_of(place, [near, swap_y(near)], near.shape[1], shape, split_x, down)


def wide(rows):
    return rows.astype(jnp.float32)


def reduce_blocks(place, mate, mine, split_x):
    both = [mine, swap_core(mate)]
    if split_x:
        quarter = mine.shape[2] // 2

        def part(rows, side):
            return wide(lax.dynamic_slice_in_dim(rows, side * quarter, quarter, 2))

        sent = sum(part(rows, 1 - place.x) for rows in both).astype(jnp.bfloat16)
        came = swap_x(sent)

        def half_y(index):
            return sum(pick(part(rows, place.x), index) for rows in both) + wide(pick(came, index))
    else:

        def half_y(index):
            return sum(wide(pick(rows, index)) for rows in both)

    came_y = swap_y(half_y(1 - place.y).astype(jnp.bfloat16))
    near = half_y(place.y) + wide(came_y)
    total = pick(near, place.z)
    for step in (1, 2, 3):
        sent = pick(near, (place.z + step) % 4).astype(jnp.bfloat16)
        total = total + wide(turn_z(sent, step))
    total = total.astype(jnp.bfloat16)
    if split_x:
        far = swap_x(total)
        total = jnp.where(
            place.x == 0, jnp.concatenate([total, far]), jnp.concatenate([far, total])
        )
    else:
        total = (wide(total) + wide(swap_x(total))).astype(jnp.bfloat16)
    far = swap_core(total)
    return jnp.where(
        place.c == 0, jnp.concatenate([total, far]), jnp.concatenate([far, total])
    ).astype(jnp.float32)


def document_columns(doc_ids):
    hot = (doc_ids[:, None] == jnp.arange(128)[None, :]) & (jnp.arange(128) < 3)[None, :]
    other = (~hot) & (jnp.arange(128) < 3)[None, :]
    return (
        jnp.where(other, MASKED_SCORE, 0.0).astype(jnp.bfloat16),
        hot.astype(jnp.bfloat16),
    )


def head_part(rows, side):
    column = lax.broadcasted_iota(jnp.int32, rows.shape, 1)
    inside = column < HEAD_DIM if side == 0 else column >= HEAD_DIM
    return jnp.where(inside, rows, jnp.zeros_like(rows))


def attend_kernel(q_ref, k_ref, v_ref, qx_ref, kx_ref, ctx_ref, lse_ref, out_scr):
    rows = q_ref.shape[0]
    step = min(256, rows)
    keys = jnp.concatenate([k_ref[...], kx_ref[...]], axis=1)
    values_t = v_ref[...].T
    for side in range(2):
        queries = jnp.concatenate([head_part(q_ref[...], side), qx_ref[...]], axis=1)
        mine = slice(side * HEAD_DIM, (side + 1) * HEAD_DIM)
        for at in range(0, rows, step):
            scores = wide_dot(keys, queries[at : at + step], NT)
            top = jnp.max(scores, axis=0, keepdims=True)
            weights = jnp.exp2((scores - top) * SCALE_TWO)
            total = jnp.sum(weights, axis=0, keepdims=True)
            attended = wide_dot(values_t[mine], weights.astype(jnp.bfloat16))
            out_scr[mine, at : at + step] = attended * (1.0 / total)
            lse_ref[0, side : side + 1, at : at + step] = top * SCALE_TWO + jnp.log2(total)
    ctx_ref[...] = out_scr[...].T.astype(jnp.bfloat16)


def attention_forward(queries, key_rows, value_rows, doc_columns):
    rows = queries.shape[0]
    pair = pl.BlockSpec((rows, 128), lambda h: (0, h))
    fixed = pl.BlockSpec((rows, 128), lambda h: (0, 0))
    return pl.pallas_call(
        attend_kernel,
        grid=(HEADS // 2,),
        out_shape=(
            jax.ShapeDtypeStruct((rows, D), jnp.bfloat16),
            jax.ShapeDtypeStruct((HEADS // 2, 2, rows), jnp.float32),
        ),
        in_specs=[pair, pair, pair, fixed, fixed],
        out_specs=(pair, pl.BlockSpec((1, 2, rows), lambda h: (h, 0, 0))),
        scratch_shapes=[pltpu.VMEM((128, rows), jnp.float32)],
        compiler_params=vmem(40),
        cost_estimate=pl.CostEstimate(
            flops=8 * HEADS * rows * rows * 128, bytes_accessed=8 * rows * D, transcendentals=HEADS * rows * rows
        ),
    )(queries, key_rows, value_rows, *doc_columns)


def attend_back_kernel(
    q_ref, k_ref, v_ref, do_ref, ctx_ref, lse_ref, qx_ref, kx_ref,
    dq_ref, dk_ref, dv_ref, sums_ref, dq_scr,
):
    rows = q_ref.shape[0]
    step = min(256, rows)
    grads = do_ref[...]
    product_t = (grads.astype(jnp.float32) * ctx_ref[...].astype(jnp.float32)).T
    keys_t = k_ref[...].T
    heads = []
    for side in range(2):
        mine = slice(side * HEAD_DIM, (side + 1) * HEAD_DIM)
        q_side = head_part(q_ref[...], side)
        heads.append((
            mine,
            q_side,
            jnp.concatenate([q_side, qx_ref[...]], axis=1),
            head_part(grads, side),
            jnp.sum(product_t[mine], axis=0, keepdims=True),
            lse_ref[0, side : side + 1, :],
        ))
    value_sum = jnp.zeros((1, 128), jnp.float32)
    for at in range(0, rows, step):
        here = slice(at, at + step)
        keys = jnp.concatenate([k_ref[here], kx_ref[here]], axis=1)
        key_grad = jnp.zeros((step, 128), jnp.float32)
        value_grad = jnp.zeros((step, 128), jnp.float32)
        for mine, q_side, queries, do_side, delta, lse in heads:
            weights = jnp.exp2(wide_dot(keys, queries, NT) * SCALE_TWO - lse)
            grad_weights = wide_dot(v_ref[here], do_side, NT)
            grad_scores = (weights * (grad_weights - delta)).astype(jnp.bfloat16)
            value_grad += wide_dot(weights.astype(jnp.bfloat16), do_side)
            key_grad += wide_dot(grad_scores, q_side)
            query_grad = wide_dot(keys_t[mine, here], grad_scores)
            if at == 0:
                dq_scr[mine] = query_grad
            else:
                dq_scr[mine] += query_grad
        dk_ref[here] = (key_grad * 0.125).astype(jnp.bfloat16)
        value_low = value_grad.astype(jnp.bfloat16)
        dv_ref[here] = value_low
        value_sum += jnp.sum(value_low.astype(jnp.float32), axis=0, keepdims=True)
    query_low = (dq_scr[...].T * 0.125).astype(jnp.bfloat16)
    dq_ref[...] = query_low
    query_sum = jnp.sum(query_low.astype(jnp.float32), axis=0, keepdims=True)
    sums_ref[...] = jnp.concatenate([query_sum, value_sum], axis=0)


def attention_backward(queries, key_rows, value_rows, doc_columns, grad_context, context, log_total):
    rows = queries.shape[0]
    pair = pl.BlockSpec((rows, 128), lambda h: (0, h))
    fixed = pl.BlockSpec((rows, 128), lambda h: (0, 0))
    like = jax.ShapeDtypeStruct((rows, D), jnp.bfloat16)
    return pl.pallas_call(
        attend_back_kernel,
        grid=(HEADS // 2,),
        out_shape=(like, like, like, jax.ShapeDtypeStruct((2, D), jnp.float32)),
        in_specs=[pair] * 5 + [pl.BlockSpec((1, 2, rows), lambda h: (h, 0, 0)), fixed, fixed],
        out_specs=(pair, pair, pair, pl.BlockSpec((2, 128), lambda h: (0, h))),
        scratch_shapes=[pltpu.VMEM((128, rows), jnp.float32)],
        compiler_params=vmem(40),
        cost_estimate=pl.CostEstimate(
            flops=20 * HEADS * rows * rows * 128, bytes_accessed=18 * rows * D, transcendentals=HEADS * rows * rows
        ),
    )(queries, key_rows, value_rows, grad_context, context, log_total, *doc_columns)


def gelu_kernel(x_ref, w_ref, b_ref, act_ref, slope_ref):
    inner = wide_dot(x_ref[...], w_ref[...]) + b_ref[...].astype(jnp.float32)
    phi = 0.5 + 0.5 * lax.erf(inner * math.sqrt(0.5))
    bell = jnp.exp(inner * inner * -0.5) * (1.0 / math.sqrt(2.0 * math.pi))
    act_ref[...] = (inner * phi).astype(jnp.bfloat16)
    slope_ref[...] = (phi + inner * bell).astype(jnp.bfloat16)


def gelu_forward(rows, w_in, b_in):
    count, units = rows.shape[0], w_in.shape[1]
    tile = 512
    column = pl.BlockSpec((count, tile), lambda j: (0, j))
    like = jax.ShapeDtypeStruct((count, units), jnp.bfloat16)
    return pl.pallas_call(
        gelu_kernel,
        grid=(units // tile,),
        out_shape=(like, like),
        in_specs=[
            pl.BlockSpec((count, D), lambda j: (0, 0)),
            pl.BlockSpec((D, tile), lambda j: (0, j)),
            pl.BlockSpec((1, tile), lambda j: (0, j)),
        ],
        out_specs=(column, column),
        compiler_params=vmem(40),
        cost_estimate=pl.CostEstimate(
            flops=2 * count * D * units, bytes_accessed=4 * count * units, transcendentals=2 * count * units
        ),
    )(rows, w_in, b_in.reshape(1, -1))


def inner_grad_kernel(g_ref, w_ref, slope_ref, out_ref, sum_ref):
    grad = wide_dot(g_ref[...], w_ref[...], NT) * slope_ref[...].astype(jnp.float32)
    low = grad.astype(jnp.bfloat16)
    out_ref[...] = low
    sum_ref[...] = jnp.sum(low.astype(jnp.float32), axis=0, keepdims=True)


def inner_backward(grad_mlp, w_down, slope):
    count, units = slope.shape
    tile = 512
    column = pl.BlockSpec((count, tile), lambda j: (0, j))
    return pl.pallas_call(
        inner_grad_kernel,
        grid=(units // tile,),
        out_shape=(
            jax.ShapeDtypeStruct((count, units), jnp.bfloat16),
            jax.ShapeDtypeStruct((1, units), jnp.float32),
        ),
        in_specs=[
            pl.BlockSpec((count, D), lambda j: (0, 0)),
            pl.BlockSpec((tile, D), lambda j: (j, 0)),
            column,
        ],
        out_specs=(column, pl.BlockSpec((1, tile), lambda j: (0, j))),
        compiler_params=vmem(40),
        cost_estimate=pl.CostEstimate(
            flops=2 * count * D * units, bytes_accessed=6 * count * units, transcendentals=0
        ),
    )(grad_mlp, w_down, slope)


def weight_grad_kernel(down, side_ref, a_ref, b_ref, out_ref):
    total = wide_dot(a_ref[...], b_ref[...], TN).astype(jnp.bfloat16)
    for part in range(total.shape[0] // ROWS):
        piece = total[part * ROWS : (part + 1) * ROWS]
        if down:
            out_ref[0, 0, part] = piece
        else:
            out_ref[part % 2, part // 2, 0] = piece


def weight_grad(side, left, right, down=False):
    count = left.shape[0]
    if down:
        grid, nb = (8,), 4
        specs = [
            pl.BlockSpec((count, LANES), lambda f, s: (0, f)),
            pl.BlockSpec((count, LANES), lambda f, s: (0, s[0])),
        ]
        out = pl.BlockSpec((1, 1, nb, ROWS, LANES), lambda f, s: (lax.rem(f, 2), lax.div(f, 2), 0, 0, 0))
    else:
        nb = right.shape[1] // LANES // 2
        grid = (nb,)
        specs = [
            pl.BlockSpec((count, D), lambda j, s: (0, 0)),
            pl.BlockSpec((count, LANES), lambda j, s: (0, s[0] * nb + j)),
        ]
        out = pl.BlockSpec((2, 4, 1, ROWS, LANES), lambda j, s: (0, 0, j, 0, 0))
    return pl.pallas_call(
        functools.partial(weight_grad_kernel, down),
        grid_spec=pltpu.PrefetchScalarGridSpec(
            num_scalar_prefetch=1, grid=grid, in_specs=specs, out_specs=out
        ),
        out_shape=jax.ShapeDtypeStruct((2, 4, nb, ROWS, LANES), jnp.bfloat16),
        compiler_params=vmem(40),
        cost_estimate=pl.CostEstimate(
            flops=2 * count * D * nb * LANES, bytes_accessed=count * (D + nb * LANES) * 2, transcendentals=0
        ),
    )(side.reshape(1), left, right)


def small_to_blocks(grad_vectors, grad_b_in, place):
    vectors = jnp.pad(
        grad_vectors.reshape(8, 4, 2, ROWS).transpose(2, 1, 0, 3),
        ((0, 0), (0, 0), (0, 8), (0, LANES - ROWS)),
    )
    biases = jnp.pad(
        grad_b_in.reshape(4, 2, 1, LANES).transpose(1, 0, 2, 3), ((0, 0), (0, 0), (0, 15), (0, 0))
    )
    vectors, biases = vectors.astype(jnp.bfloat16), biases.astype(jnp.bfloat16)
    return (
        jnp.where(place.c == 0, biases, vectors),
        jnp.where(place.c == 0, vectors, biases),
    )


class Staged:
    def __init__(self, w_qkv, vectors, w_attn_out, w_in, b_in, w_down):
        self.place = place = Place()
        small = jnp.pad(
            jnp.concatenate([b_in[None], jnp.pad(vectors, ((0, 0), (0, LANES - ROWS)))]),
            ((0, 7), (0, 0)),
        )
        own = own_blocks(to_blocks(w_qkv, False), place, False)
        own = jnp.concatenate([own.reshape(-1, LANES), small])[None]
        near = gather_z(own)
        near_y = swap_y(near)
        self.qkv = gather_rest_of(place, [near, near_y], 3, (D, 3 * D), False, False)
        edge = [near[:, 0, 3 * ROWS :], near_y[:, 0, 3 * ROWS :]]
        edge = jnp.stack(
            [
                jnp.stack(
                    [
                        jnp.where(place.y == y, *(pick(e, (place.z - z) % 4) for e in edge))
                        for y in range(2)
                    ]
                )
                for z in range(4)
            ]
        )
        self.b_in = edge[:, :, 0].reshape(-1)
        self.vectors = edge[:, :, 1:9, :ROWS].transpose(2, 0, 1, 3).reshape(8, D)
        blocks = after(own_blocks(to_blocks(w_attn_out, False), place, False), near)
        near_out = gather_z(blocks)
        blocks = after(own_blocks(to_blocks(w_in, False), place, True), near)
        near_in = gather_z(blocks)
        blocks = after(own_blocks(to_blocks(w_down, True), place, True), near_out, near_in)
        near_down = gather_z(blocks)
        self.out = gather_rest(place, near_out, (D, D), False, False)
        self.w_in = gather_rest(place, near_in, (D, 4 * D), True, False)
        self.down = gather_rest(place, near_down, (4 * D, D), True, True)

    def reduce(self, left, right, down=False, split_x=False, small=None):
        place = self.place
        mate = weight_grad(1 - place.c, left, right, down)
        mine = weight_grad(place.c, left, right, down)
        if small is not None:
            nb = mate.shape[2]
            mate, mine = (
                jnp.concatenate([rows.reshape(2, 4, nb * ROWS, LANES), edge], axis=2)[:, :, None]
                for rows, edge in zip((mate, mine), small_to_blocks(*small, place), strict=True)
            )
        shard = reduce_blocks(place, mate, mine, split_x)
        if small is not None:
            edge = shard[:, nb * ROWS :]
            shard = shard[:, : nb * ROWS].reshape(2 * nb, ROWS, LANES)
        if down:
            shard = shard.reshape(2, 4, ROWS, LANES).transpose(1, 2, 0, 3).reshape(LANES, D)
        else:
            shard = shard.transpose(1, 0, 2).reshape(ROWS, -1)
        return shard if small is None else (shard, edge[0, :8, :ROWS], edge[1, 0])


class Plain:
    def __init__(self, w_qkv, vectors, w_attn_out, w_in, b_in, w_down):
        def whole(rows, axis=0):
            return lax.all_gather(rows, "fsdp", axis=axis, tiled=True)

        self.qkv, self.vectors, self.out = whole(w_qkv), whole(vectors, 1), whole(w_attn_out)
        self.w_in, self.b_in, self.down = whole(w_in), whole(b_in), whole(w_down)

    def own(self, total, axis=0):
        shard = lax.psum_scatter(total, "fsdp", scatter_dimension=axis, tiled=True)
        return lax.psum(shard.astype(jnp.bfloat16), "rep").astype(jnp.float32)

    def reduce(self, left, right, down=False, split_x=False, small=None):
        shard = self.own(wide_dot(left, right, TN))
        return shard if small is None else (shard, self.own(small[0], 1), self.own(small[1]))


def body(staged, tokens, lengths, w_qkv, vectors, w_attn_out, w_in, b_in, w_down, cotangent):
    row_count = tokens.shape[0]
    valid_rows, doc_ids = layout(lengths[0], row_count)
    doc_columns = document_columns(doc_ids)
    weights = (Staged if staged else Plain)(w_qkv, vectors, w_attn_out, w_in, b_in, w_down)
    vector_wide = weights.vectors.astype(jnp.float32)
    projected = jnp.dot(tokens, weights.qkv, preferred_element_type=jnp.float32)
    queries = (projected[:, :D] + vector_wide[0]).astype(jnp.bfloat16)
    key_rows = projected[:, D : 2 * D].astype(jnp.bfloat16)
    value_rows = (projected[:, 2 * D :] + vector_wide[1]).astype(jnp.bfloat16)
    context, log_total = attention_forward(queries, key_rows, value_rows, doc_columns)
    attn_branch = jnp.dot(context, weights.out, preferred_element_type=jnp.float32) + vector_wide[2]
    first_norm, normed_one, inverse_one = norm_forward(
        tokens.astype(jnp.float32) + attn_branch, vector_wide[3], vector_wide[4]
    )
    first_low = first_norm.astype(jnp.bfloat16)
    active, slope = gelu_forward(first_low, weights.w_in, weights.b_in)
    mlp_branch = jnp.dot(active, weights.down, preferred_element_type=jnp.float32) + vector_wide[5]
    second_norm, normed_two, inverse_two = norm_forward(
        first_norm + mlp_branch, vector_wide[6], vector_wide[7]
    )
    layer_out = jnp.where(valid_rows[:, None], second_norm, 0.0).astype(jnp.bfloat16)
    grad_out = jnp.where(valid_rows[:, None], cotangent.astype(jnp.float32), 0.0)
    grad_two, gain_two, shift_two = norm_backward(grad_out, normed_two, inverse_two, vector_wide[6])
    grad_mlp = grad_two.astype(jnp.bfloat16)
    down_shard = weights.reduce(active, grad_mlp, down=True, split_x=False)
    grad_inner, grad_b_in = inner_backward(grad_mlp, weights.down, slope)
    in_shard = weights.reduce(first_low, grad_inner, split_x=True)
    grad_b_down = jnp.sum(grad_mlp.astype(jnp.float32), axis=0)
    grad_first = grad_two + wide_dot(grad_inner, weights.w_in, NT)
    grad_one, gain_one, shift_one = norm_backward(
        grad_first, normed_one, inverse_one, vector_wide[3]
    )
    grad_attn = grad_one.astype(jnp.bfloat16)
    grad_context = wide_dot(grad_attn, weights.out, NT).astype(jnp.bfloat16)
    out_shard = weights.reduce(context, grad_attn)
    query_low, key_low, value_low, column_sums = attention_backward(
        queries, key_rows, value_rows, doc_columns, grad_context, context, log_total
    )
    grad_proj = jnp.concatenate([query_low, key_low, value_low], axis=1)
    grad_vectors = jnp.concatenate(
        [
            column_sums,
            jnp.stack(
                [
                    jnp.sum(grad_attn.astype(jnp.float32), axis=0),
                    gain_one,
                    shift_one,
                    grad_b_down,
                    gain_two,
                    shift_two,
                ]
            ),
        ]
    )
    qkv_shard, vector_shard, bias_shard = weights.reduce(
        tokens, grad_proj, small=(grad_vectors, grad_b_in.reshape(-1))
    )
    grad_tokens = (grad_one + wide_dot(grad_proj, weights.qkv, NT)).astype(jnp.bfloat16)
    return (
        layer_out,
        grad_tokens,
        qkv_shard,
        vector_shard,
        out_shard,
        in_shard,
        bias_shard,
        down_shard,
    )


def solution(mesh):
    staged = mesh.shape["fsdp"] == 8 and mesh.shape["rep"] == 4
    return jax.shard_map(
        functools.partial(body, staged),
        mesh=mesh,
        in_specs=(
            P(("fsdp", "rep"), None),
            P(("fsdp", "rep"), None),
            P("fsdp", None),
            P(None, "fsdp"),
            P("fsdp", None),
            P("fsdp", None),
            P("fsdp"),
            P("fsdp", None),
            P(("fsdp", "rep"), None),
        ),
        out_specs=(
            P(("fsdp", "rep"), None),
            P(("fsdp", "rep"), None),
            P("fsdp", None),
            P(None, "fsdp"),
            P("fsdp", None),
            P("fsdp", None),
            P("fsdp"),
            P("fsdp", None),
        ),
        check_vma=False,
    )
```

```python
import functools
import math

import jax
import jax.numpy as jnp
from jax import lax
from jax.experimental import pallas as pl
from jax.experimental.pallas import tpu as pltpu
from jax.sharding import PartitionSpec as P

D = 768
HEADS = 12
HEAD_DIM = 64
BLOCK = 128

NORM_EPS = 1e-12
MASKED_SCORE = -1e30
SCALE_TWO = 0.125 * math.log2(math.e)
MIB = 1 << 20
CHEAP = 8

NT = (((1,), (1,)), ((), ()))
TN = (((0,), (0,)), ((), ()))


def wide_dot(left, right, dims=(((1,), (0,)), ((), ()))):
    return lax.dot_general(left, right, dims, preferred_element_type=jnp.float32)


def vmem(mib):
    return pltpu.CompilerParams(vmem_limit_bytes=mib * MIB)


def cost(flops, bytes_accessed, transcendentals=0):
    return pl.CostEstimate(
        flops=flops // CHEAP, bytes_accessed=bytes_accessed // CHEAP, transcendentals=transcendentals // CHEAP
    )


def layout(length_row, row_count):
    first_len = length_row[0]
    second_len = length_row[1]
    second_start = (first_len + BLOCK - 1) // BLOCK * BLOCK
    positions = jnp.arange(row_count, dtype=jnp.int32)
    in_first = positions < first_len
    in_second = (positions >= second_start) & (positions < second_start + second_len)
    doc_ids = jnp.where(in_first, 0, jnp.where(in_second, 1, 2)).astype(jnp.int32)
    return (in_first | in_second, doc_ids)


def norm_forward(hidden, gain_row, shift_row):
    centre = jnp.mean(hidden, axis=-1, keepdims=True)
    spread = jnp.mean(jnp.square(hidden - centre), axis=-1, keepdims=True)
    inverse = lax.rsqrt(spread + NORM_EPS)
    normed = (hidden - centre) * inverse
    return (normed * gain_row + shift_row, normed, inverse)


def norm_backward_rows(grad_rows, normed, inverse, gain_row):
    scaled = grad_rows * gain_row
    return inverse * (
        scaled
        - jnp.mean(scaled, axis=-1, keepdims=True)
        - normed * jnp.mean(scaled * normed, axis=-1, keepdims=True)
    )


def norm_backward(grad_rows, normed, inverse, gain_row):
    grad_in = norm_backward_rows(grad_rows, normed, inverse, gain_row)
    return (grad_in, jnp.sum(grad_rows * normed, axis=0), jnp.sum(grad_rows, axis=0))


LANES = 384
ROWS = 96
HALF = ROWS // 2


class Place:
    def __init__(self):
        fsdp, rep = lax.axis_index("fsdp"), lax.axis_index("rep")
        self.z, self.y = fsdp // 2, fsdp % 2
        self.x, self.c = rep // 2, rep % 2
        self.scalars = jnp.stack([self.z, self.y, self.x, self.c]).astype(jnp.int32)


def swap_core(rows):
    return lax.ppermute(rows, "rep", [(i, i ^ 1) for i in range(4)])


def swap_x(rows):
    return lax.ppermute(rows, "rep", [(i, i ^ 2) for i in range(4)])


def swap_y(rows):
    return lax.ppermute(rows, "fsdp", [(i, i ^ 1) for i in range(8)])


def turn_z(rows, step):
    return lax.ppermute(rows, "fsdp", [(i, (i + 2 * step) % 8) for i in range(8)])


def pick(rows, index):
    return lax.dynamic_index_in_dim(rows, index, 0, keepdims=False)


def after(rows, *others):
    return lax.optimization_barrier((rows, *others))[0]


def wide(rows):
    return rows.astype(jnp.float32)


def low(rows):
    return rows.astype(jnp.bfloat16)


def turned(own):
    return [turn_z(own, step) for step in (1, 2, 3)]


def to_blocks(shard, place, split_x=False, down=False):
    if down:
        blocks = shard.reshape(4, 2, HALF, 2, LANES).transpose(1, 3, 0, 2, 4).reshape(2, 8, HALF, LANES)
    else:
        blocks = shard.reshape(2, HALF, -1, LANES).transpose(0, 2, 1, 3)
    blocks = pick(blocks, place.c)
    if split_x:
        nb = blocks.shape[0] // 2
        blocks = lax.dynamic_slice_in_dim(blocks, place.x * nb, nb, 0)
    return blocks


def assemble(near_ref, pieces, full_ref, nb):
    z, y, c = near_ref[0], near_ref[1], near_ref[3]
    for p, piece in enumerate(pieces):
        core = 1 - c if p >> 1 else c
        for k in range(4):
            f = lax.rem(z + 4 - k, 4) * 2 + (1 - y if p & 1 else y)
            row = pl.multiple_of(f * ROWS + core * HALF, HALF)
            for j in range(nb):
                full_ref[pl.ds(row, HALF), j * LANES : (j + 1) * LANES] = piece[
                    k, j * HALF : (j + 1) * HALF
                ]


def assemble_down(near_ref, pieces, full_ref):
    z, y, c = near_ref[0], near_ref[1], near_ref[3]
    for p, piece in enumerate(pieces):
        core = 1 - c if p >> 1 else c
        for k in range(4):
            f = lax.rem(z + 4 - k, 4) * 2 + (1 - y if p & 1 else y)
            for j in range(8):
                row = pl.multiple_of(f * (4 * ROWS) + j % 4 * ROWS + core * HALF, HALF)
                col = j // 4 * LANES
                full_ref[pl.ds(row, HALF), col : col + LANES] = piece[k, j * HALF : (j + 1) * HALF]


def rest_kernel(near_ref, *refs):
    in_ref, out_ref = refs[-2:]
    z, y, x, c = near_ref[0], near_ref[1], near_ref[2], near_ref[3]
    for p, piece in enumerate(refs[:-2]):
        core = 1 - c if p >> 2 else c
        side = 1 - x if (p >> 1) & 1 else x
        for k in range(4):
            f = lax.rem(z + 4 - k, 4) * 2 + (1 - y if p & 1 else y)
            row = pl.ds(pl.multiple_of(f * ROWS + core * HALF, HALF), HALF)
            for j in range(4):
                col = pl.ds(pl.multiple_of((side * 4 + j) * LANES, LANES), LANES)
                in_ref[row, col] = piece[k, j * HALF : (j + 1) * HALF]
            col = pl.ds(pl.multiple_of(side * LANES, LANES), LANES)
            out_ref[row, col] = piece[k, 4 * HALF : 5 * HALF]


def down_kernel(near_ref, *refs):
    assemble_down(near_ref, refs[:-1], refs[-1])


def put_together(kernel, near, pieces, shapes):
    whole = pl.BlockSpec(memory_space=pltpu.VMEM)
    return pl.pallas_call(
        kernel,
        out_shape=tuple(jax.ShapeDtypeStruct(shape, jnp.bfloat16) for shape in shapes),
        in_specs=[pl.BlockSpec(memory_space=pltpu.SMEM)] + [whole] * len(pieces),
        out_specs=(whole,) * len(shapes),
        compiler_params=vmem(16),
        cost_estimate=cost(0, 4 * sum(math.prod(shape) for shape in shapes), 0),
    )(near, *pieces)


class Reduction:
    def __init__(self, place, mate, mine, split_x=False):
        self.place, self.split_x = place, split_x
        self.both = [mine, swap_core(mate)]
        self.others = []

    def part(self, rows, side):
        half = rows.shape[2] // 2
        return wide(lax.dynamic_slice_in_dim(rows, side * half, half, 2))

    def send_x(self):
        place = self.place
        if self.split_x:
            self.for_x = low(sum(self.part(rows, 1 - place.x) for rows in self.both))
            self.from_x = swap_x(self.for_x)
        return self

    def half_y(self, index):
        if not self.split_x:
            return sum(wide(pick(rows, index)) for rows in self.both)
        kept = sum(pick(self.part(rows, self.place.x), index) for rows in self.both)
        return kept + wide(pick(self.from_x, index))

    def send_y(self):
        self.for_y = low(self.half_y(1 - self.place.y))
        self.from_y = swap_y(self.for_y)
        return self

    def send_z(self):
        near = self.half_y(self.place.y) + wide(self.from_y)
        self.kept = pick(near, self.place.z)
        self.for_z = [low(pick(near, (self.place.z + step) % 4)) for step in (1, 2, 3)]
        self.from_z = [turn_z(rows, step) for step, rows in zip((1, 2, 3), self.for_z, strict=True)]
        return self

    def send_last_x(self):
        self.total = low(self.kept + sum(wide(rows) for rows in self.from_z))
        self.far = swap_x(self.total)
        return self

    def send_last_core(self):
        if self.split_x:
            both = jnp.concatenate([self.total, self.far]), jnp.concatenate([self.far, self.total])
            self.total = jnp.where(self.place.x == 0, *both)
        else:
            self.total = low(wide(self.total) + wide(self.far))
        self.far = swap_core(self.total)
        return self

    def send_last(self):
        self.total = low(self.kept + sum(wide(rows) for rows in self.from_z))
        self.others = [lax.ppermute(self.total, "rep", [(i, i ^ at) for i in range(4)]) for at in (2, 1, 3)]
        return self

    def finish(self):
        if self.others:
            x, core, both = (wide(rows) for rows in self.others)
            mine, theirs = wide(self.total) + x, core + both
            return jnp.where(self.place.c == 0, jnp.stack([mine, theirs]), jnp.stack([theirs, mine]))
        both = jnp.stack([self.total, self.far]), jnp.stack([self.far, self.total])
        return wide(jnp.where(self.place.c == 0, *both))


def from_blocks(parts, nb, down=False):
    if down:
        blocks = parts.reshape(2, 2, 4, HALF, LANES)
        return blocks.transpose(2, 0, 3, 1, 4).reshape(LANES, 2 * LANES)
    return parts.reshape(2, nb, HALF, LANES).transpose(0, 2, 1, 3).reshape(ROWS, nb * LANES)


def document_columns(doc_ids):
    hot = (doc_ids[:, None] == jnp.arange(128)[None, :]) & (jnp.arange(128) < 3)[None, :]
    other = (~hot) & (jnp.arange(128) < 3)[None, :]
    return (
        jnp.where(other, MASKED_SCORE, 0.0).astype(jnp.bfloat16),
        hot.astype(jnp.bfloat16),
    )


def head_part(rows, side):
    column = lax.broadcasted_iota(jnp.int32, rows.shape, 1)
    inside = column < HEAD_DIM if side == 0 else column >= HEAD_DIM
    return jnp.where(inside, rows, jnp.zeros_like(rows))


def attend_kernel(qkv_ref, qx_ref, kx_ref, ctx_ref, lse_ref, out_scr):
    rows = qkv_ref.shape[0]
    step = min(256, rows)
    keys = jnp.concatenate([qkv_ref[:, 128:256], kx_ref[...]], axis=1)
    values_t = qkv_ref[:, 256:].T
    for side in range(2):
        queries = jnp.concatenate([head_part(qkv_ref[:, :128], side), qx_ref[...]], axis=1)
        mine = slice(side * HEAD_DIM, (side + 1) * HEAD_DIM)
        for at in range(0, rows, step):
            scores = wide_dot(keys, queries[at : at + step], NT)
            top = jnp.max(scores, axis=0, keepdims=True)
            weights = jnp.exp2((scores - top) * SCALE_TWO)
            total = jnp.sum(weights, axis=0, keepdims=True)
            attended = wide_dot(values_t[mine], weights.astype(jnp.bfloat16))
            out_scr[mine, at : at + step] = attended * (1.0 / total)
            lse_ref[0, side : side + 1, at : at + step] = top * SCALE_TWO + jnp.log2(total)
    ctx_ref[...] = out_scr[...].T.astype(jnp.bfloat16)


def attention_forward(projected, doc_columns, first, pairs=3):
    rows = projected.shape[0]
    fixed = pl.BlockSpec((rows, 128), lambda h: (0, 0))
    return pl.pallas_call(
        attend_kernel,
        grid=(pairs,),
        out_shape=(
            jax.ShapeDtypeStruct((rows, pairs * 128), jnp.bfloat16),
            jax.ShapeDtypeStruct((pairs, 2, rows), jnp.float32),
        ),
        in_specs=[pl.BlockSpec((rows, 384), lambda h: (0, first + h)), fixed, fixed],
        out_specs=(
            pl.BlockSpec((rows, 128), lambda h: (0, h)),
            pl.BlockSpec((1, 2, rows), lambda h: (h, 0, 0)),
        ),
        scratch_shapes=[pltpu.VMEM((128, rows), jnp.float32)],
        compiler_params=vmem(32),
        cost_estimate=cost(16 * pairs * rows * rows * 128, 8 * rows * pairs * 128, 2 * pairs * rows * rows),
    )(projected, *doc_columns)


def attend_back_kernel(
    qkv_ref, do_ref, ctx_ref, lse_ref, qx_ref, kx_ref, out_ref, sums_ref, dq_scr
):
    rows = qkv_ref.shape[0]
    step = min(256, rows)
    grads = do_ref[...]
    product_t = (wide(grads) * wide(ctx_ref[...])).T
    keys_t = qkv_ref[:, 128:256].T
    heads = []
    for side in range(2):
        mine = slice(side * HEAD_DIM, (side + 1) * HEAD_DIM)
        q_side = head_part(qkv_ref[:, :128], side)
        heads.append((
            mine,
            q_side,
            jnp.concatenate([q_side, qx_ref[...]], axis=1),
            head_part(grads, side),
            jnp.sum(product_t[mine], axis=0, keepdims=True),
            lse_ref[0, side : side + 1, :],
        ))
    value_sum = jnp.zeros((1, 128), jnp.float32)
    for at in range(0, rows, step):
        here = slice(at, at + step)
        keys = jnp.concatenate([qkv_ref[here, 128:256], kx_ref[here]], axis=1)
        key_grad = jnp.zeros((step, 128), jnp.float32)
        value_grad = jnp.zeros((step, 128), jnp.float32)
        for mine, q_side, queries, do_side, delta, lse in heads:
            weights = jnp.exp2(wide_dot(keys, queries, NT) * SCALE_TWO - lse)
            grad_weights = wide_dot(qkv_ref[here, 256:], do_side, NT)
            grad_scores = (weights * (grad_weights - delta)).astype(jnp.bfloat16)
            value_grad += wide_dot(weights.astype(jnp.bfloat16), do_side)
            key_grad += wide_dot(grad_scores, q_side)
            query_grad = wide_dot(keys_t[mine, here], grad_scores)
            if at == 0:
                dq_scr[mine] = query_grad
            else:
                dq_scr[mine] += query_grad
        out_ref[here, 128:256] = low(key_grad * 0.125)
        value_low = low(value_grad)
        out_ref[here, 256:] = value_low
        value_sum += jnp.sum(wide(value_low), axis=0, keepdims=True)
    query_low = low(dq_scr[...].T * 0.125)
    out_ref[:, :128] = query_low
    query_sum = jnp.sum(wide(query_low), axis=0, keepdims=True)
    sums_ref[...] = jnp.concatenate([query_sum, value_sum], axis=0)


def attention_backward(projected, doc_columns, grad_context, context, log_total, pairs, own_first, first):
    rows = projected.shape[0]
    fixed = pl.BlockSpec((rows, 128), lambda h: (0, 0))
    return pl.pallas_call(
        attend_back_kernel,
        grid=(pairs,),
        out_shape=(
            jax.ShapeDtypeStruct((rows, pairs * 384), jnp.bfloat16),
            jax.ShapeDtypeStruct((2, pairs * 128), jnp.float32),
        ),
        in_specs=[
            pl.BlockSpec((rows, 384), lambda h: (0, first + h)),
            pl.BlockSpec((rows, 128), lambda h: (0, first + h)),
            pl.BlockSpec((rows, 128), lambda h: (0, own_first + h)),
            pl.BlockSpec((1, 2, rows), lambda h: (own_first + h, 0, 0)),
            fixed,
            fixed,
        ],
        out_specs=(
            pl.BlockSpec((rows, 384), lambda h: (0, h)),
            pl.BlockSpec((2, 128), lambda h: (0, h)),
        ),
        scratch_shapes=[pltpu.VMEM((128, rows), jnp.float32)],
        compiler_params=vmem(32),
        cost_estimate=cost(40 * pairs * rows * rows * 128, 18 * rows * pairs * 128, 2 * pairs * rows * rows),
    )(projected, grad_context, context, log_total, *doc_columns)


def gelu_tile(x_ref, w_ref, b_ref, act_ref, slope_ref):
    inner = wide_dot(x_ref[...], w_ref) + wide(b_ref[...])
    phi = 0.5 + 0.5 * lax.erf(inner * math.sqrt(0.5))
    bell = jnp.exp(inner * inner * -0.5) * (1.0 / math.sqrt(2.0 * math.pi))
    act_ref[...] = low(inner * phi)
    slope_ref[...] = low(phi + inner * bell)


def gelu_kernel(x_ref, w_ref, b_ref, act_ref, slope_ref):
    gelu_tile(x_ref, w_ref[...], b_ref, act_ref, slope_ref)


def gelu_forward(rows, w_in, b_in):
    count, units = rows.shape[0], w_in.shape[1]
    tile = 512
    column = pl.BlockSpec((count, tile), lambda j: (0, j))
    like = jax.ShapeDtypeStruct((count, units), jnp.bfloat16)
    return pl.pallas_call(
        gelu_kernel,
        grid=(units // tile,),
        out_shape=(like, like),
        in_specs=[
            pl.BlockSpec((count, D), lambda j: (0, 0)),
            pl.BlockSpec((D, tile), lambda j: (0, j)),
            pl.BlockSpec((1, tile), lambda j: (0, j)),
        ],
        out_specs=(column, column),
        compiler_params=vmem(32),
        cost_estimate=cost(2 * count * D * units, 4 * count * units, 2 * count * units),
    )(rows, w_in, b_in.reshape(1, -1))


def inner_grad_kernel(g_ref, w_ref, slope_ref, out_ref, sum_ref):
    grad = wide_dot(g_ref[...], w_ref[...], NT) * slope_ref[...].astype(jnp.float32)
    low = grad.astype(jnp.bfloat16)
    out_ref[...] = low
    sum_ref[...] = jnp.sum(low.astype(jnp.float32), axis=0, keepdims=True)


def inner_backward(grad_mlp, w_down, slope):
    count, units = slope.shape
    tile = 512
    column = pl.BlockSpec((count, tile), lambda j: (0, j))
    return pl.pallas_call(
        inner_grad_kernel,
        grid=(units // tile,),
        out_shape=(
            jax.ShapeDtypeStruct((count, units), jnp.bfloat16),
            jax.ShapeDtypeStruct((1, units), jnp.float32),
        ),
        in_specs=[
            pl.BlockSpec((count, D), lambda j: (0, 0)),
            pl.BlockSpec((tile, D), lambda j: (j, 0)),
            column,
        ],
        out_specs=(column, pl.BlockSpec((1, tile), lambda j: (0, j))),
        compiler_params=vmem(32),
        cost_estimate=cost(2 * count * D * units, 6 * count * units, 0),
    )(grad_mlp, w_down, slope)


def keep_halves(total, c, mate_ref, mine_ref, where_of):
    for part in range(total.shape[0] // ROWS):
        for j in range(total.shape[1] // LANES):
            first, second = (
                total[part * ROWS + at : part * ROWS + at + HALF, j * LANES : (j + 1) * LANES]
                for at in (0, HALF)
            )
            to = where_of(part, j)
            mate_ref[to] = jnp.where(c == 0, second, first)
            mine_ref[to] = jnp.where(c == 0, first, second)


def feed_back_kernel(
    near_ref, mlp_ref, low_ref, active_ref, slope_ref, down_ref, in_ref,
    first_ref, bias_ref, down_mate, down_mine, in_mate, in_mine, low_t,
):
    c = near_ref[3]
    start = pl.program_id(0) == 0

    @pl.when(start)
    def _():
        low_t[...] = low_ref[...].T

    grad_inner = low(wide_dot(mlp_ref[...], down_ref[...], NT) * wide(slope_ref[...]))
    bias_ref[...] = jnp.sum(wide(grad_inner), axis=0, keepdims=True)

    def of_in(part, j):
        return (part % 2, part // 2, slice(j * HALF, (j + 1) * HALF))

    def of_down(part, j):
        return (part // 4, 0, slice((j * 4 + part % 4) * HALF, (j * 4 + part % 4 + 1) * HALF))

    keep_halves(low(wide_dot(low_t[...], grad_inner)), c, in_mate, in_mine, of_in)
    keep_halves(low(wide_dot(active_ref[...], mlp_ref[...], TN)), c, down_mate, down_mine, of_down)
    back = wide_dot(grad_inner, in_ref[...], NT)

    @pl.when(start)
    def _():
        first_ref[...] = back

    @pl.when(jnp.logical_not(start))
    def _():
        first_ref[...] += back


def feed_backward(near, grad_mlp, first_low, active, slope, down_full, in_full):
    count, units = active.shape
    tile = 2 * LANES
    rows = 8 * HALF
    fixed = pl.BlockSpec((count, D), lambda u: (0, 0), pipeline_mode=pl.Buffered(1))
    column = pl.BlockSpec((count, tile), lambda u: (0, u))
    like = jax.ShapeDtypeStruct((2, 4, rows, LANES), jnp.bfloat16)
    down_out = pl.BlockSpec((2, 1, rows, LANES), lambda u: (0, u, 0, 0))
    in_out = pl.BlockSpec((2, 4, 2 * HALF, LANES), lambda u: (0, 0, u, 0))
    return pl.pallas_call(
        feed_back_kernel,
        grid=(units // tile,),
        in_specs=[
            pl.BlockSpec(memory_space=pltpu.SMEM),
            fixed,
            fixed,
            column,
            column,
            pl.BlockSpec((tile, D), lambda u: (u, 0)),
            pl.BlockSpec((D, tile), lambda u: (0, u)),
        ],
        out_specs=(
            pl.BlockSpec((count, D), lambda u: (0, 0)),
            pl.BlockSpec((1, tile), lambda u: (0, u)),
            down_out, down_out, in_out, in_out,
        ),
        out_shape=(
            jax.ShapeDtypeStruct((count, D), jnp.float32),
            jax.ShapeDtypeStruct((1, units), jnp.float32),
            like, like, like, like,
        ),
        scratch_shapes=[pltpu.VMEM((D, count), jnp.bfloat16)],
        compiler_params=vmem(48),
        cost_estimate=cost(8 * count * D * units, 8 * count * units),
    )(near, grad_mlp, first_low, active, slope, down_full, in_full)


def qkv_grad_kernel(many, near_ref, *refs):
    left_ref, rights, edges = refs[0], refs[1 : 1 + many], refs[1 + many : -2]
    mate_ref, mine_ref = refs[-2:]
    c = near_ref[3]
    right = jnp.concatenate([ref[...] for ref in rights], axis=1)
    blocks = right.shape[1] // LANES

    def where_of(part, j):
        return (part % 2, part // 2, slice(j * HALF, (j + 1) * HALF))

    keep_halves(low(wide_dot(left_ref[...], right, TN)), c, mate_ref, mine_ref, where_of)
    for ref, edge in zip((mate_ref, mine_ref), edges, strict=True):
        ref[:, :, blocks * HALF :] = edge[...]


def out_grad_kernel(near_ref, left_ref, right_ref, edge_left, edge_right, mate_ref, mine_ref):
    c = near_ref[3]

    def where_of(part, j):
        return (part % 2, part // 2, slice(j * HALF, (j + 1) * HALF))

    keep_halves(low(wide_dot(left_ref[...], right_ref[...], TN)), c, mate_ref, mine_ref, where_of)
    blocks = right_ref.shape[1] // LANES

    def edge_of(part, j):
        return (part % 2, part // 2, slice((blocks + j) * HALF, (blocks + j + 1) * HALF))

    keep_halves(low(wide_dot(edge_left[...], edge_right[...], TN)), c, mate_ref, mine_ref, edge_of)


def whole_grad(kernel, near, arrays, rows, flops):
    like = jax.ShapeDtypeStruct((2, 4, rows, LANES), jnp.bfloat16)
    whole = pl.BlockSpec(memory_space=pltpu.VMEM)
    return pl.pallas_call(
        kernel,
        in_specs=[pl.BlockSpec(memory_space=pltpu.SMEM)] + [whole] * len(arrays),
        out_specs=(whole, whole),
        out_shape=(like, like),
        compiler_params=vmem(32),
        cost_estimate=cost(flops, sum(2 * a.size for a in arrays), 0),
    )(near, *arrays)


def lo_and_out_grad(near, left, right, out_left, out_right):
    rows = (right.shape[1] + out_right.shape[1]) // LANES * HALF
    flops = 2 * left.shape[0] * D * (right.shape[1] + out_right.shape[1])
    return whole_grad(out_grad_kernel, near, [left, right, out_left, out_right], rows, flops)


def hi_grad(near, left, rights, edges):
    width = sum(right.shape[1] for right in rights)
    rows = width // LANES * HALF + edges[0].shape[2]
    kernel = functools.partial(qkv_grad_kernel, len(rights))
    return whole_grad(kernel, near, [left, *rights, *edges], rows, 2 * left.shape[0] * D * width)


def project_kernel(nb, near_ref, tokens_ref, *refs):
    pieces = refs[:4]
    full_ref, out_ref, vec_ref, b_ref = refs[4:]
    small = sum(
        wide(piece[k, nb * HALF : nb * HALF + 24]) for piece in pieces[:2] for k in range(4)
    )
    vec_ref[:, :LANES] = small[:8]
    vec_ref[:, LANES:] = small[8:16]
    for f in range(8):
        b_ref[:, f * LANES : (f + 1) * LANES] = small[16 + f : 17 + f]
    assemble(near_ref, pieces, full_ref, nb)
    for j in range(nb):
        here = slice(j * LANES, (j + 1) * LANES)
        pair = slice(j * 128, (j + 1) * 128)
        bias = jnp.concatenate(
            [vec_ref[0:1, pair], jnp.zeros((1, 128), jnp.float32), vec_ref[1:2, pair]], axis=1
        )
        out_ref[:, here] = low(wide_dot(tokens_ref[...], full_ref[:, here]) + bias)


def project(near, tokens, pieces, nb):
    count = tokens.shape[0]
    whole = pl.BlockSpec(memory_space=pltpu.VMEM)
    return pl.pallas_call(
        functools.partial(project_kernel, nb),
        out_shape=(
            jax.ShapeDtypeStruct((D, nb * LANES), jnp.bfloat16),
            jax.ShapeDtypeStruct((count, nb * LANES), jnp.bfloat16),
            jax.ShapeDtypeStruct((8, D), jnp.float32),
            jax.ShapeDtypeStruct((1, 4 * D), jnp.float32),
        ),
        in_specs=[pl.BlockSpec(memory_space=pltpu.SMEM)] + [whole] * (1 + len(pieces)),
        out_specs=(whole,) * 4,
        compiler_params=vmem(32),
        cost_estimate=cost(2 * count * D * nb * LANES, 6 * count * D),
    )(near, tokens, *pieces)


def pairs_of(rows):
    lead = rows.shape[:-1]
    return jnp.moveaxis(rows.reshape(*lead, 3, HEADS // 2, 128), -3, -2).reshape(*lead, 3 * D)


def of_pairs(rows):
    lead = rows.shape[:-1]
    return jnp.moveaxis(rows.reshape(*lead, HEADS // 2, 3, 128), -3, -2).reshape(*lead, 3 * D)


def small_to_blocks(grad_vectors, grad_b_in, place):
    vectors = jnp.pad(
        grad_vectors.reshape(8, 4, 2, ROWS).transpose(2, 1, 0, 3),
        ((0, 0), (0, 0), (0, 8), (0, LANES - ROWS)),
    )
    biases = jnp.pad(
        grad_b_in.reshape(4, 2, 1, LANES).transpose(1, 0, 2, 3), ((0, 0), (0, 0), (0, 15), (0, 0))
    )
    vectors, biases = low(vectors), low(biases)
    return (
        jnp.where(place.c == 0, biases, vectors),
        jnp.where(place.c == 0, vectors, biases),
    )


def layer_front(tokens, context, out_weight, vector_wide):
    attn_branch = wide_dot(context, out_weight) + vector_wide[2]
    return norm_forward(wide(tokens) + attn_branch, vector_wide[3], vector_wide[4])


def layer_end(active, down, first_norm, vector_wide, valid_rows, cotangent):
    mlp_branch = wide_dot(active, down) + vector_wide[5]
    second_norm, normed_two, inverse_two = norm_forward(
        first_norm + mlp_branch, vector_wide[6], vector_wide[7]
    )
    layer_out = low(jnp.where(valid_rows[:, None], second_norm, 0.0))
    grad_out = jnp.where(valid_rows[:, None], wide(cotangent), 0.0)
    return (layer_out, *norm_backward(grad_out, normed_two, inverse_two, vector_wide[6]))


def staged_body(tokens, lengths, w_qkv, vectors, w_attn_out, w_in, b_in, w_down, cotangent):
    place = Place()
    near = place.scalars
    valid_rows, doc_ids = layout(lengths[0], tokens.shape[0])
    doc_columns = document_columns(doc_ids)

    fsdp = lax.axis_index("fsdp")
    small = lax.dynamic_update_slice(jnp.zeros((8, D), jnp.bfloat16), vectors, (0, fsdp * ROWS))
    small = jnp.concatenate([small[:, :LANES], small[:, LANES:]])
    own_b = lax.dynamic_update_slice(jnp.zeros((16, LANES), jnp.bfloat16), b_in[None], (fsdp, 0))
    own = jnp.concatenate([to_blocks(pairs_of(w_qkv), place).reshape(-1, LANES), small, own_b])
    qkv = jnp.stack([own, *turned(own)])
    qkv_y = swap_y(qkv)
    qkv_pieces = [qkv, qkv_y, swap_core(qkv), swap_core(qkv_y)]
    own = jnp.concatenate(
        [
            to_blocks(w_in, place, True).reshape(-1, LANES),
            to_blocks(w_attn_out, place, True).reshape(-1, LANES),
            to_blocks(w_down, place, down=True).reshape(-1, LANES),
        ]
    )
    own = after(own, qkv)
    came = turned(own)
    w_qkv_full, projected, vector_wide, b_full = project(
        near, after(tokens, came[0], came[2]), qkv_pieces, HEADS // 2
    )
    context_lo, total_lo = attention_forward(projected, doc_columns, 0)
    both = [own, came[0], after(came[1], context_lo), came[2]]
    rest = [jnp.stack([rows[: 5 * HALF] for rows in both])]
    down = jnp.stack([rows[5 * HALF :] for rows in both])
    rest += [swap_y(rest[0]), swap_x(rest[0])]
    context_hi, total_hi = attention_forward(after(projected, context_lo, rest[0], down), doc_columns, 3)
    rest[1:] = after(rest[1:], context_hi)
    down_y = swap_y(after(down, rest[1]))
    rest.append(swap_x(rest[1]))
    rest += [swap_core(piece) for piece in rest]
    in_full, out_full = put_together(rest_kernel, near, rest, [(D, 4 * D), (D, D)])
    context = jnp.concatenate([context_lo, context_hi], axis=1)
    first_norm, normed_one, inverse_one = layer_front(tokens, context, out_full, vector_wide)
    first_low = low(first_norm)
    active, slope = gelu_forward(first_low, in_full, b_full.reshape(-1))
    down_y = after(down_y, active)
    down_pieces = [down, down_y, swap_core(down), swap_core(down_y)]
    (down_full,) = put_together(down_kernel, near, down_pieces, [(4 * D, D)])
    layer_out, grad_two, gain_two, shift_two = layer_end(
        active, down_full, first_norm, vector_wide, valid_rows, cotangent
    )

    grad_mlp = low(grad_two)
    back_first, grad_b_in, *parts = feed_backward(
        near, grad_mlp, first_low, active, slope, down_full, in_full
    )
    down_sum = Reduction(place, *parts[:2])
    in_sum = Reduction(place, *parts[2:], split_x=True)
    grad_one, gain_one, shift_one = norm_backward(
        grad_two + back_first, normed_one, inverse_one, vector_wide[3]
    )
    grad_attn = low(grad_one)
    grad_context = low(wide_dot(grad_attn, out_full, NT))
    down_sum.send_x().send_y()
    in_sum.send_x()

    def back_of(projected, context, total, pairs, own_first, first, *others):
        return attention_backward(
            projected, doc_columns, after(grad_context, *others), context, total, pairs, own_first, first
        )

    back_a, sums_a = back_of(projected, context_lo, total_lo, 2, 0, 0, in_sum.for_x, down_sum.for_y)
    down_sum.from_y = after(down_sum.from_y, back_a)
    down_sum.send_z()
    back_b, sums_b = back_of(projected, context_lo, total_lo, 1, 2, 2, back_a, down_sum.for_z)
    in_sum.from_x = after(in_sum.from_x, back_b)
    in_sum.send_y()
    back_lo = jnp.concatenate([back_a, back_b], axis=1)
    lo_sum = Reduction(
        place, *lo_and_out_grad(near, tokens, after(back_lo, in_sum.for_y), context, grad_attn)
    )
    back_3, sums_3 = back_of(projected, context_hi, total_hi, 1, 0, 3, lo_sum.both[0], in_sum.for_y)
    lo_sum.both[1], in_sum.from_y = after((lo_sum.both[1], in_sum.from_y), back_3)
    lo_sum.send_y()
    in_sum.send_z()
    back_4, sums_4 = back_of(
        projected, context_hi, total_hi, 1, 1, 4, back_3, lo_sum.for_y, in_sum.for_z
    )
    down_sum.from_z = after(down_sum.from_z, back_4)
    down_sum.send_last_x()
    back_5, sums_5 = back_of(projected, context_hi, total_hi, 1, 2, 5, back_4, down_sum.total)
    lo_sum.from_y, down_sum.far = after((lo_sum.from_y, down_sum.far), back_5)
    grad_vectors = jnp.concatenate(
        [
            jnp.concatenate([sums_a, sums_b, sums_3, sums_4, sums_5], axis=1),
            jnp.stack(
                [
                    jnp.sum(wide(grad_attn), axis=0),
                    gain_one,
                    shift_one,
                    jnp.sum(wide(grad_mlp), axis=0),
                    gain_two,
                    shift_two,
                ]
            ),
        ]
    )
    hi_sum = Reduction(
        place,
        *hi_grad(
            near, tokens, [back_3, back_4, back_5], small_to_blocks(grad_vectors, grad_b_in, place)
        ),
    )
    lo_sum.from_y = after(lo_sum.from_y, hi_sum.both[0])
    lo_sum.send_z()
    hi_sum.both[1] = after(hi_sum.both[1], lo_sum.for_z)
    hi_sum.send_y()
    in_sum.from_z, down_sum.far = after((in_sum.from_z, down_sum.far), hi_sum.for_y)
    in_sum.send_last_x()
    down_sum.send_last_core()
    back = jnp.concatenate([back_lo, back_3, back_4, back_5], axis=1)
    grad_tokens = low(
        grad_one + wide_dot(after(back, in_sum.total, down_sum.total), w_qkv_full, NT)
    )
    hi_sum.from_y = after(hi_sum.from_y, grad_tokens)
    hi_sum.send_z()
    lo_sum.from_z, in_sum.far = after((lo_sum.from_z, in_sum.far), hi_sum.for_z)
    in_sum.send_last_core()
    lo_sum.send_last()
    hi_sum.from_z = after(hi_sum.from_z, lo_sum.total, in_sum.total)
    hi_sum.send_last()
    in_part, down_part, lo_part, hi_part = (
        total.finish() for total in (in_sum, down_sum, lo_sum, hi_sum)
    )
    qkv_shard = jnp.concatenate(
        [from_blocks(lo_part[:, : 3 * HALF], 3), from_blocks(hi_part[:, : 3 * HALF], 3)], axis=1
    )
    small = hi_part[:, 3 * HALF :]
    return (
        layer_out,
        grad_tokens,
        of_pairs(qkv_shard),
        small[0, :8, :ROWS],
        from_blocks(lo_part[:, 3 * HALF :], 2),
        from_blocks(in_part, 8),
        small[1, 0],
        from_blocks(down_part, 8, True),
    )


def plain_body(tokens, lengths, w_qkv, vectors, w_attn_out, w_in, b_in, w_down, cotangent):
    def whole(rows, axis=0):
        return lax.all_gather(rows, "fsdp", axis=axis, tiled=True)

    def own(total, axis=0):
        shard = lax.psum_scatter(total, "fsdp", scatter_dimension=axis, tiled=True)
        return wide(lax.psum(low(shard), "rep"))

    valid_rows, doc_ids = layout(lengths[0], tokens.shape[0])
    doc_columns = document_columns(doc_ids)
    qkv_full, out_full, in_full, down_full = whole(w_qkv), whole(w_attn_out), whole(w_in), whole(w_down)
    vector_wide = wide(whole(vectors, 1))
    bias = jnp.concatenate([vector_wide[0], jnp.zeros((D,), jnp.float32), vector_wide[1]])
    projected = pairs_of(low(wide_dot(tokens, qkv_full) + bias))
    context, log_total = attention_forward(projected, doc_columns, 0, HEADS // 2)
    first_norm, normed_one, inverse_one = layer_front(tokens, context, out_full, vector_wide)
    first_low = low(first_norm)
    active, slope = gelu_forward(first_low, in_full, whole(b_in))
    layer_out, grad_two, gain_two, shift_two = layer_end(
        active, down_full, first_norm, vector_wide, valid_rows, cotangent
    )
    grad_mlp = low(grad_two)
    grad_inner, grad_b_in = inner_backward(grad_mlp, down_full, slope)
    grad_first = grad_two + wide_dot(grad_inner, in_full, NT)
    grad_one, gain_one, shift_one = norm_backward(
        grad_first, normed_one, inverse_one, vector_wide[3]
    )
    grad_attn = low(grad_one)
    grad_context = low(wide_dot(grad_attn, out_full, NT))
    back, column_sums = attention_backward(
        projected, doc_columns, grad_context, context, log_total, HEADS // 2, 0, 0
    )
    back = of_pairs(back)
    edge = [
        jnp.sum(wide(grad_attn), axis=0), gain_one, shift_one, jnp.sum(wide(grad_mlp), axis=0), gain_two, shift_two
    ]
    return (
        layer_out,
        low(grad_one + wide_dot(back, qkv_full, NT)),
        own(wide_dot(tokens, back, TN)),
        own(jnp.concatenate([column_sums, jnp.stack(edge)]), 1),
        own(wide_dot(context, grad_attn, TN)),
        own(wide_dot(first_low, grad_inner, TN)),
        own(grad_b_in.reshape(-1)),
        own(wide_dot(active, grad_mlp, TN)),
    )


def solution(mesh):
    staged = mesh.shape["fsdp"] == 8 and mesh.shape["rep"] == 4
    return jax.shard_map(
        staged_body if staged else plain_body,
        mesh=mesh,
        in_specs=(
            P(("fsdp", "rep"), None),
            P(("fsdp", "rep"), None),
            P("fsdp", None),
            P(None, "fsdp"),
            P("fsdp", None),
            P("fsdp", None),
            P("fsdp"),
            P("fsdp", None),
            P(("fsdp", "rep"), None),
        ),
        out_specs=(
            P(("fsdp", "rep"), None),
            P(("fsdp", "rep"), None),
            P("fsdp", None),
            P(None, "fsdp"),
            P("fsdp", None),
            P("fsdp", None),
            P("fsdp"),
            P("fsdp", None),
        ),
        check_vma=False,
    )
```

```python
import functools
import math

import jax
import jax.numpy as jnp
from jax import lax
from jax.experimental import pallas as pl
from jax.experimental.pallas import tpu as pltpu
from jax.sharding import PartitionSpec as P

D = 768
HEADS = 12
HEAD_DIM = 64
BLOCK = 128

NORM_EPS = 1e-12
MASKED_SCORE = -1e30
SCALE_TWO = 0.125 * math.log2(math.e)
MIB = 1 << 20
CHEAP = 8

NT = (((1,), (1,)), ((), ()))
TN = (((0,), (0,)), ((), ()))


def wide_dot(left, right, dims=(((1,), (0,)), ((), ()))):
    return lax.dot_general(left, right, dims, preferred_element_type=jnp.float32)


def vmem(mib):
    return pltpu.CompilerParams(vmem_limit_bytes=mib * MIB)


def cost(flops, bytes_accessed, transcendentals=0):
    return pl.CostEstimate(
        flops=flops // CHEAP, bytes_accessed=bytes_accessed // CHEAP, transcendentals=transcendentals // CHEAP
    )


def at_once(shape):
    return pl.BlockSpec(shape, lambda i: (0,) * len(shape), pipeline_mode=pl.Buffered(1))


def layout(length_row, row_count):
    first_len = length_row[0]
    second_len = length_row[1]
    second_start = (first_len + BLOCK - 1) // BLOCK * BLOCK
    positions = jnp.arange(row_count, dtype=jnp.int32)
    in_first = positions < first_len
    in_second = (positions >= second_start) & (positions < second_start + second_len)
    doc_ids = jnp.where(in_first, 0, jnp.where(in_second, 1, 2)).astype(jnp.int32)
    return (in_first | in_second, doc_ids)


def norm_forward(hidden, gain_row, shift_row):
    centre = jnp.mean(hidden, axis=-1, keepdims=True)
    spread = jnp.mean(jnp.square(hidden - centre), axis=-1, keepdims=True)
    inverse = lax.rsqrt(spread + NORM_EPS)
    normed = (hidden - centre) * inverse
    return (normed * gain_row + shift_row, normed, inverse)


def norm_backward_rows(grad_rows, normed, inverse, gain_row):
    scaled = grad_rows * gain_row
    return inverse * (
        scaled
        - jnp.mean(scaled, axis=-1, keepdims=True)
        - normed * jnp.mean(scaled * normed, axis=-1, keepdims=True)
    )


def norm_backward(grad_rows, normed, inverse, gain_row):
    grad_in = norm_backward_rows(grad_rows, normed, inverse, gain_row)
    return (grad_in, jnp.sum(grad_rows * normed, axis=0), jnp.sum(grad_rows, axis=0))


LANES = 384
ROWS = 96
HALF = ROWS // 2


class Place:
    def __init__(self):
        fsdp, rep = lax.axis_index("fsdp"), lax.axis_index("rep")
        self.z, self.y = fsdp // 2, fsdp % 2
        self.x, self.c = rep // 2, rep % 2
        self.scalars = jnp.stack([self.z, self.y, self.x, self.c]).astype(jnp.int32)


def swap_core(rows):
    return lax.ppermute(rows, "rep", [(i, i ^ 1) for i in range(4)])


def swap_x(rows):
    return lax.ppermute(rows, "rep", [(i, i ^ 2) for i in range(4)])


def swap_y(rows):
    return lax.ppermute(rows, "fsdp", [(i, i ^ 1) for i in range(8)])


def turn_z(rows, step):
    return lax.ppermute(rows, "fsdp", [(i, (i + 2 * step) % 8) for i in range(8)])


def pick(rows, index):
    return lax.dynamic_index_in_dim(rows, index, 0, keepdims=False)


def after(rows, *others):
    return lax.optimization_barrier((rows, *others))[0]


def wide(rows):
    return rows.astype(jnp.float32)


def low(rows):
    return rows.astype(jnp.bfloat16)


def turned(own):
    return [turn_z(own, step) for step in (1, 2, 3)]


def to_blocks(shard, place, split_x=False, down=False):
    if down:
        blocks = shard.reshape(4, 2, HALF, 2, LANES).transpose(1, 3, 0, 2, 4).reshape(2, 8, HALF, LANES)
    else:
        blocks = shard.reshape(2, HALF, -1, LANES).transpose(0, 2, 1, 3)
    blocks = pick(blocks, place.c)
    if split_x:
        nb = blocks.shape[0] // 2
        blocks = lax.dynamic_slice_in_dim(blocks, place.x * nb, nb, 0)
    return blocks


def assemble(near_ref, pieces, full_ref, nb):
    z, y, c = near_ref[0], near_ref[1], near_ref[3]
    for p, piece in enumerate(pieces):
        core = 1 - c if p >> 1 else c
        for k in range(4):
            f = lax.rem(z + 4 - k, 4) * 2 + (1 - y if p & 1 else y)
            row = pl.multiple_of(f * ROWS + core * HALF, HALF)
            for j in range(nb):
                full_ref[pl.ds(row, HALF), j * LANES : (j + 1) * LANES] = piece[
                    k, j * HALF : (j + 1) * HALF
                ]


def assemble_down(near_ref, pieces, full_ref):
    z, y, c = near_ref[0], near_ref[1], near_ref[3]
    for p, piece in enumerate(pieces):
        core = 1 - c if p >> 1 else c
        for k in range(4):
            f = lax.rem(z + 4 - k, 4) * 2 + (1 - y if p & 1 else y)
            for j in range(8):
                row = pl.multiple_of(f * (4 * ROWS) + j % 4 * ROWS + core * HALF, HALF)
                col = j // 4 * LANES
                full_ref[pl.ds(row, HALF), col : col + LANES] = piece[k, j * HALF : (j + 1) * HALF]


def rest_kernel(near_ref, *refs):
    in_ref, out_ref = refs[-2:]
    z, y, x, c = near_ref[0], near_ref[1], near_ref[2], near_ref[3]
    for p, piece in enumerate(refs[:-2]):
        core = 1 - c if p >> 2 else c
        side = 1 - x if (p >> 1) & 1 else x
        for k in range(4):
            f = lax.rem(z + 4 - k, 4) * 2 + (1 - y if p & 1 else y)
            row = pl.ds(pl.multiple_of(f * ROWS + core * HALF, HALF), HALF)
            for j in range(4):
                col = pl.ds(pl.multiple_of((side * 4 + j) * LANES, LANES), LANES)
                in_ref[row, col] = piece[k, j * HALF : (j + 1) * HALF]
            col = pl.ds(pl.multiple_of(side * LANES, LANES), LANES)
            out_ref[row, col] = piece[k, 4 * HALF : 5 * HALF]


def down_kernel(near_ref, *refs):
    assemble_down(near_ref, refs[:-1], refs[-1])


def put_together(kernel, near, pieces, shapes):
    return pl.pallas_call(
        kernel,
        grid=(1,),
        out_shape=tuple(jax.ShapeDtypeStruct(shape, jnp.bfloat16) for shape in shapes),
        in_specs=[pl.BlockSpec(memory_space=pltpu.SMEM)] + [at_once(piece.shape) for piece in pieces],
        out_specs=tuple(at_once(shape) for shape in shapes),
        compiler_params=vmem(16),
        cost_estimate=cost(0, 4 * sum(math.prod(shape) for shape in shapes), 0),
    )(near, *pieces)


class Reduction:
    def __init__(self, place, mate, mine, split_x=False):
        self.place, self.split_x = place, split_x
        self.both = [mine, swap_core(mate)]

    def part(self, rows, side):
        half = rows.shape[2] // 2
        return wide(lax.dynamic_slice_in_dim(rows, side * half, half, 2))

    def send_x(self):
        place = self.place
        if self.split_x:
            self.for_x = low(sum(self.part(rows, 1 - place.x) for rows in self.both))
            self.from_x = swap_x(self.for_x)
        return self

    def half_y(self, index):
        if not self.split_x:
            return sum(wide(pick(rows, index)) for rows in self.both)
        kept = sum(pick(self.part(rows, self.place.x), index) for rows in self.both)
        return kept + wide(pick(self.from_x, index))

    def send_y(self):
        self.for_y = low(self.half_y(1 - self.place.y))
        self.from_y = swap_y(self.for_y)
        return self

    def send_z(self):
        near = self.half_y(self.place.y) + wide(self.from_y)
        self.kept = pick(near, self.place.z)
        self.for_z = [low(pick(near, (self.place.z + step) % 4)) for step in (1, 2, 3)]
        self.from_z = [turn_z(rows, step) for step, rows in zip((1, 2, 3), self.for_z, strict=True)]
        return self

    def send_last_x(self):
        self.total = low(self.kept + sum(wide(rows) for rows in self.from_z))
        self.far = swap_x(self.total)
        return self

    def send_last_core(self):
        if self.split_x:
            both = jnp.concatenate([self.total, self.far]), jnp.concatenate([self.far, self.total])
            self.total = jnp.where(self.place.x == 0, *both)
        else:
            self.total = low(wide(self.total) + wide(self.far))
        self.far = swap_core(self.total)
        return self

    def send_last(self):
        self.total = low(self.kept + sum(wide(rows) for rows in self.from_z))
        self.others = [lax.ppermute(self.total, "rep", [(i, i ^ at) for i in range(4)]) for at in (2, 1, 3)]
        return self

    def finish(self):
        both = jnp.stack([self.total, self.far]), jnp.stack([self.far, self.total])
        return wide(jnp.where(self.place.c == 0, *both))


def from_blocks(parts, nb, down=False):
    if down:
        blocks = parts.reshape(2, 2, 4, HALF, LANES)
        return blocks.transpose(2, 0, 3, 1, 4).reshape(LANES, 2 * LANES)
    return parts.reshape(2, nb, HALF, LANES).transpose(0, 2, 1, 3).reshape(ROWS, nb * LANES)


def document_columns(doc_ids):
    hot = (doc_ids[:, None] == jnp.arange(128)[None, :]) & (jnp.arange(128) < 3)[None, :]
    other = (~hot) & (jnp.arange(128) < 3)[None, :]
    return (
        jnp.where(other, MASKED_SCORE, 0.0).astype(jnp.bfloat16),
        hot.astype(jnp.bfloat16),
    )


def head_part(rows, side):
    column = lax.broadcasted_iota(jnp.int32, rows.shape, 1)
    inside = column < HEAD_DIM if side == 0 else column >= HEAD_DIM
    return jnp.where(inside, rows, jnp.zeros_like(rows))


def attend_kernel(qkv_ref, qx_ref, kx_ref, ctx_ref, lse_ref, out_scr):
    rows = qkv_ref.shape[0]
    step = min(256, rows)
    keys = jnp.concatenate([qkv_ref[:, 128:256], kx_ref[...]], axis=1)
    values_t = qkv_ref[:, 256:].T
    for side in range(2):
        queries = jnp.concatenate([head_part(qkv_ref[:, :128], side), qx_ref[...]], axis=1)
        mine = slice(side * HEAD_DIM, (side + 1) * HEAD_DIM)
        for at in range(0, rows, step):
            scores = wide_dot(keys, queries[at : at + step], NT)
            top = jnp.max(scores, axis=0, keepdims=True)
            weights = jnp.exp2((scores - top) * SCALE_TWO)
            total = jnp.sum(weights, axis=0, keepdims=True)
            attended = wide_dot(values_t[mine], weights.astype(jnp.bfloat16))
            out_scr[mine, at : at + step] = attended * (1.0 / total)
            lse_ref[0, side : side + 1, at : at + step] = top * SCALE_TWO + jnp.log2(total)
    ctx_ref[...] = out_scr[...].T.astype(jnp.bfloat16)


def attention_forward(projected, doc_columns, first, pairs=3):
    rows = projected.shape[0]
    fixed = pl.BlockSpec((rows, 128), lambda h: (0, 0))
    return pl.pallas_call(
        attend_kernel,
        grid=(pairs,),
        out_shape=(
            jax.ShapeDtypeStruct((rows, pairs * 128), jnp.bfloat16),
            jax.ShapeDtypeStruct((pairs, 2, rows), jnp.float32),
        ),
        in_specs=[pl.BlockSpec((rows, 384), lambda h: (0, first + h)), fixed, fixed],
        out_specs=(
            pl.BlockSpec((rows, 128), lambda h: (0, h)),
            pl.BlockSpec((1, 2, rows), lambda h: (h, 0, 0)),
        ),
        scratch_shapes=[pltpu.VMEM((128, rows), jnp.float32)],
        compiler_params=vmem(32),
        cost_estimate=cost(16 * pairs * rows * rows * 128, 8 * rows * pairs * 128, 2 * pairs * rows * rows),
    )(projected, *doc_columns)


def attend_back_kernel(
    qkv_ref, do_ref, ctx_ref, lse_ref, qx_ref, kx_ref, out_ref, sums_ref, dq_scr
):
    rows = qkv_ref.shape[0]
    step = min(256, rows)
    grads = do_ref[...]
    product_t = (wide(grads) * wide(ctx_ref[...])).T
    keys_t = qkv_ref[:, 128:256].T
    heads = []
    for side in range(2):
        mine = slice(side * HEAD_DIM, (side + 1) * HEAD_DIM)
        q_side = head_part(qkv_ref[:, :128], side)
        heads.append((
            mine,
            q_side,
            jnp.concatenate([q_side, qx_ref[...]], axis=1),
            head_part(grads, side),
            jnp.sum(product_t[mine], axis=0, keepdims=True),
            lse_ref[0, side : side + 1, :],
        ))
    value_sum = jnp.zeros((1, 128), jnp.float32)
    for at in range(0, rows, step):
        here = slice(at, at + step)
        keys = jnp.concatenate([qkv_ref[here, 128:256], kx_ref[here]], axis=1)
        key_grad = jnp.zeros((step, 128), jnp.float32)
        value_grad = jnp.zeros((step, 128), jnp.float32)
        for mine, q_side, queries, do_side, delta, lse in heads:
            weights = jnp.exp2(wide_dot(keys, queries, NT) * SCALE_TWO - lse)
            grad_weights = wide_dot(qkv_ref[here, 256:], do_side, NT)
            grad_scores = (weights * (grad_weights - delta)).astype(jnp.bfloat16)
            value_grad += wide_dot(weights.astype(jnp.bfloat16), do_side)
            key_grad += wide_dot(grad_scores, q_side)
            query_grad = wide_dot(keys_t[mine, here], grad_scores)
            if at == 0:
                dq_scr[mine] = query_grad
            else:
                dq_scr[mine] += query_grad
        out_ref[here, 128:256] = low(key_grad * 0.125)
        value_low = low(value_grad)
        out_ref[here, 256:] = value_low
        value_sum += jnp.sum(wide(value_low), axis=0, keepdims=True)
    query_low = low(dq_scr[...].T * 0.125)
    out_ref[:, :128] = query_low
    query_sum = jnp.sum(wide(query_low), axis=0, keepdims=True)
    sums_ref[...] = jnp.concatenate([query_sum, value_sum], axis=0)


def attention_backward(projected, doc_columns, grad_context, context, log_total, pairs, own_first, first):
    rows = projected.shape[0]
    fixed = pl.BlockSpec((rows, 128), lambda h: (0, 0))
    return pl.pallas_call(
        attend_back_kernel,
        grid=(pairs,),
        out_shape=(
            jax.ShapeDtypeStruct((rows, pairs * 384), jnp.bfloat16),
            jax.ShapeDtypeStruct((2, pairs * 128), jnp.float32),
        ),
        in_specs=[
            pl.BlockSpec((rows, 384), lambda h: (0, first + h)),
            pl.BlockSpec((rows, 128), lambda h: (0, first + h)),
            pl.BlockSpec((rows, 128), lambda h: (0, own_first + h)),
            pl.BlockSpec((1, 2, rows), lambda h: (own_first + h, 0, 0)),
            fixed,
            fixed,
        ],
        out_specs=(
            pl.BlockSpec((rows, 384), lambda h: (0, h)),
            pl.BlockSpec((2, 128), lambda h: (0, h)),
        ),
        scratch_shapes=[pltpu.VMEM((128, rows), jnp.float32)],
        compiler_params=vmem(32),
        cost_estimate=cost(40 * pairs * rows * rows * 128, 18 * rows * pairs * 128, 2 * pairs * rows * rows),
    )(projected, grad_context, context, log_total, *doc_columns)


def gelu_tile(x_ref, w_ref, b_ref, act_ref, slope_ref):
    inner = wide_dot(x_ref[...], w_ref) + wide(b_ref[...])
    phi = 0.5 + 0.5 * lax.erf(inner * math.sqrt(0.5))
    bell = jnp.exp(inner * inner * -0.5) * (1.0 / math.sqrt(2.0 * math.pi))
    act_ref[...] = low(inner * phi)
    slope_ref[...] = low(phi + inner * bell)


def gelu_kernel(x_ref, w_ref, b_ref, act_ref, slope_ref):
    gelu_tile(x_ref, w_ref[...], b_ref, act_ref, slope_ref)


def gelu_forward(rows, w_in, b_in):
    count, units = rows.shape[0], w_in.shape[1]
    tile = 512
    column = pl.BlockSpec((count, tile), lambda j: (0, j))
    like = jax.ShapeDtypeStruct((count, units), jnp.bfloat16)
    return pl.pallas_call(
        gelu_kernel,
        grid=(units // tile,),
        out_shape=(like, like),
        in_specs=[
            pl.BlockSpec((count, D), lambda j: (0, 0)),
            pl.BlockSpec((D, tile), lambda j: (0, j)),
            pl.BlockSpec((1, tile), lambda j: (0, j)),
        ],
        out_specs=(column, column),
        compiler_params=vmem(32),
        cost_estimate=cost(2 * count * D * units, 4 * count * units, 2 * count * units),
    )(rows, w_in, b_in.reshape(1, -1))


def inner_grad_kernel(g_ref, w_ref, slope_ref, out_ref, sum_ref):
    grad = wide_dot(g_ref[...], w_ref[...], NT) * slope_ref[...].astype(jnp.float32)
    low = grad.astype(jnp.bfloat16)
    out_ref[...] = low
    sum_ref[...] = jnp.sum(low.astype(jnp.float32), axis=0, keepdims=True)


def inner_backward(grad_mlp, w_down, slope):
    count, units = slope.shape
    tile = 512
    column = pl.BlockSpec((count, tile), lambda j: (0, j))
    return pl.pallas_call(
        inner_grad_kernel,
        grid=(units // tile,),
        out_shape=(
            jax.ShapeDtypeStruct((count, units), jnp.bfloat16),
            jax.ShapeDtypeStruct((1, units), jnp.float32),
        ),
        in_specs=[
            pl.BlockSpec((count, D), lambda j: (0, 0)),
            pl.BlockSpec((tile, D), lambda j: (j, 0)),
            column,
        ],
        out_specs=(column, pl.BlockSpec((1, tile), lambda j: (0, j))),
        compiler_params=vmem(32),
        cost_estimate=cost(2 * count * D * units, 6 * count * units, 0),
    )(grad_mlp, w_down, slope)


def keep_halves(total, c, mate_ref, mine_ref, where_of):
    for part in range(total.shape[0] // ROWS):
        for j in range(total.shape[1] // LANES):
            first, second = (
                total[part * ROWS + at : part * ROWS + at + HALF, j * LANES : (j + 1) * LANES]
                for at in (0, HALF)
            )
            to = where_of(part, j)
            mate_ref[to] = jnp.where(c == 0, second, first)
            mine_ref[to] = jnp.where(c == 0, first, second)


def feed_back_kernel(
    near_ref, mlp_ref, low_ref, active_ref, slope_ref, down_ref, in_ref,
    first_ref, bias_ref, down_mate, down_mine, in_mate, in_mine, low_t,
):
    c = near_ref[3]
    start = pl.program_id(0) == 0

    @pl.when(start)
    def _():
        low_t[...] = low_ref[...].T

    grad_inner = low(wide_dot(mlp_ref[...], down_ref[...], NT) * wide(slope_ref[...]))
    bias_ref[...] = jnp.sum(wide(grad_inner), axis=0, keepdims=True)

    def of_in(part, j):
        return (part % 2, part // 2, slice(j * HALF, (j + 1) * HALF))

    def of_down(part, j):
        return (part // 4, 0, slice((j * 4 + part % 4) * HALF, (j * 4 + part % 4 + 1) * HALF))

    keep_halves(low(wide_dot(low_t[...], grad_inner)), c, in_mate, in_mine, of_in)
    keep_halves(low(wide_dot(active_ref[...], mlp_ref[...], TN)), c, down_mate, down_mine, of_down)
    back = wide_dot(grad_inner, in_ref[...], NT)

    @pl.when(start)
    def _():
        first_ref[...] = back

    @pl.when(jnp.logical_not(start))
    def _():
        first_ref[...] += back


def feed_backward(near, grad_mlp, first_low, active, slope, down_full, in_full):
    count, units = active.shape
    tile = 2 * LANES
    rows = 8 * HALF
    fixed = pl.BlockSpec((count, D), lambda u: (0, 0), pipeline_mode=pl.Buffered(1))
    column = pl.BlockSpec((count, tile), lambda u: (0, u))
    like = jax.ShapeDtypeStruct((2, 4, rows, LANES), jnp.bfloat16)
    down_out = pl.BlockSpec((2, 1, rows, LANES), lambda u: (0, u, 0, 0))
    in_out = pl.BlockSpec((2, 4, 2 * HALF, LANES), lambda u: (0, 0, u, 0))
    return pl.pallas_call(
        feed_back_kernel,
        grid=(units // tile,),
        in_specs=[
            pl.BlockSpec(memory_space=pltpu.SMEM),
            fixed,
            fixed,
            column,
            column,
            pl.BlockSpec((tile, D), lambda u: (u, 0)),
            pl.BlockSpec((D, tile), lambda u: (0, u)),
        ],
        out_specs=(
            pl.BlockSpec((count, D), lambda u: (0, 0)),
            pl.BlockSpec((1, tile), lambda u: (0, u)),
            down_out, down_out, in_out, in_out,
        ),
        out_shape=(
            jax.ShapeDtypeStruct((count, D), jnp.float32),
            jax.ShapeDtypeStruct((1, units), jnp.float32),
            like, like, like, like,
        ),
        scratch_shapes=[pltpu.VMEM((D, count), jnp.bfloat16)],
        compiler_params=vmem(48),
        cost_estimate=cost(8 * count * D * units, 8 * count * units),
    )(near, grad_mlp, first_low, active, slope, down_full, in_full)


def qkv_grad_kernel(many, near_ref, *refs):
    left_ref, rights, edges = refs[0], refs[1 : 1 + many], refs[1 + many : -2]
    mate_ref, mine_ref = refs[-2:]
    c = near_ref[3]
    right = jnp.concatenate([ref[...] for ref in rights], axis=1)
    blocks = right.shape[1] // LANES

    def where_of(part, j):
        return (part % 2, part // 2, slice(j * HALF, (j + 1) * HALF))

    keep_halves(low(wide_dot(left_ref[...], right, TN)), c, mate_ref, mine_ref, where_of)
    for ref, edge in zip((mate_ref, mine_ref), edges, strict=True):
        ref[:, :, blocks * HALF :] = edge[...]


def out_grad_kernel(near_ref, left_ref, right_ref, edge_left, edge_right, mate_ref, mine_ref):
    c = near_ref[3]

    def where_of(part, j):
        return (part % 2, part // 2, slice(j * HALF, (j + 1) * HALF))

    keep_halves(low(wide_dot(left_ref[...], right_ref[...], TN)), c, mate_ref, mine_ref, where_of)
    blocks = right_ref.shape[1] // LANES

    def edge_of(part, j):
        return (part % 2, part // 2, slice((blocks + j) * HALF, (blocks + j + 1) * HALF))

    keep_halves(low(wide_dot(edge_left[...], edge_right[...], TN)), c, mate_ref, mine_ref, edge_of)


def whole_grad(kernel, near, arrays, rows, flops, mib=32):
    like = jax.ShapeDtypeStruct((2, 4, rows, LANES), jnp.bfloat16)
    return pl.pallas_call(
        kernel,
        grid=(1,),
        in_specs=[pl.BlockSpec(memory_space=pltpu.SMEM)] + [at_once(a.shape) for a in arrays],
        out_specs=(at_once(like.shape),) * 2,
        out_shape=(like, like),
        compiler_params=vmem(mib),
        cost_estimate=cost(flops, sum(2 * a.size for a in arrays), 0),
    )(near, *arrays)


def lo_and_out_grad(near, left, right, out_left, out_right):
    rows = (right.shape[1] + out_right.shape[1]) // LANES * HALF
    flops = 2 * left.shape[0] * D * (right.shape[1] + out_right.shape[1])
    return whole_grad(out_grad_kernel, near, [left, right, out_left, out_right], rows, flops)


def hi_grad(near, left, rights, edges):
    width = sum(right.shape[1] for right in rights)
    rows = width // LANES * HALF + edges[0].shape[2]
    kernel = functools.partial(qkv_grad_kernel, len(rights))
    return whole_grad(kernel, near, [left, *rights, *edges], rows, 2 * left.shape[0] * D * width, 60)


def project_kernel(nb, near_ref, tokens_ref, *refs):
    pieces = refs[:4]
    full_ref, out_ref, vec_ref, b_ref = refs[4:]
    small = sum(
        wide(piece[k, nb * HALF : nb * HALF + 24]) for piece in pieces[:2] for k in range(4)
    )
    vec_ref[:, :LANES] = small[:8]
    vec_ref[:, LANES:] = small[8:16]
    for f in range(8):
        b_ref[:, f * LANES : (f + 1) * LANES] = small[16 + f : 17 + f]
    assemble(near_ref, pieces, full_ref, nb)
    for j in range(nb):
        here = slice(j * LANES, (j + 1) * LANES)
        pair = slice(j * 128, (j + 1) * 128)
        bias = jnp.concatenate(
            [vec_ref[0:1, pair], jnp.zeros((1, 128), jnp.float32), vec_ref[1:2, pair]], axis=1
        )
        out_ref[:, here] = low(wide_dot(tokens_ref[...], full_ref[:, here]) + bias)


def project(near, tokens, pieces, nb):
    count = tokens.shape[0]
    out_shape = (
        jax.ShapeDtypeStruct((D, nb * LANES), jnp.bfloat16),
        jax.ShapeDtypeStruct((count, nb * LANES), jnp.bfloat16),
        jax.ShapeDtypeStruct((8, D), jnp.float32),
        jax.ShapeDtypeStruct((1, 4 * D), jnp.float32),
    )
    return pl.pallas_call(
        functools.partial(project_kernel, nb),
        grid=(1,),
        out_shape=out_shape,
        in_specs=[pl.BlockSpec(memory_space=pltpu.SMEM)]
        + [at_once(a.shape) for a in (tokens, *pieces)],
        out_specs=tuple(at_once(like.shape) for like in out_shape),
        compiler_params=vmem(32),
        cost_estimate=cost(2 * count * D * nb * LANES, 6 * count * D),
    )(near, tokens, *pieces)


def last_kernel(near_ref, *refs):
    qkv_ref, out_ref, vec_ref, b_ref = refs[-4:]
    c = near_ref[3]
    first_pair = 0
    for total, x, core, both in (refs[:4], refs[4:8]):
        mine, theirs = wide(total[...]) + wide(x[...]), wide(core[...]) + wide(both[...])
        parts = jnp.where(c == 0, mine, theirs), jnp.where(c == 0, theirs, mine)
        for at, part in enumerate(parts):
            rows = slice(at * HALF, (at + 1) * HALF)
            for j in range(3):
                for kind in range(3):
                    col = kind * D + (first_pair + j) * 128
                    qkv_ref[rows, col : col + 128] = part[
                        j * HALF : (j + 1) * HALF, kind * 128 : (kind + 1) * 128
                    ]
            if first_pair == 0:
                for j in range(2):
                    out_ref[rows, j * LANES : (j + 1) * LANES] = part[(3 + j) * HALF : (4 + j) * HALF]
            elif at == 0:
                vec_ref[...] = part[3 * HALF : 3 * HALF + 8, :ROWS]
            else:
                b_ref[...] = part[3 * HALF : 3 * HALF + 1]
        first_pair += 3


def last_sums(near, lo_sum, hi_sum):
    arrays = [lo_sum.total, *lo_sum.others, hi_sum.total, *hi_sum.others]
    shapes = [(ROWS, 3 * D), (ROWS, D), (8, ROWS), (1, LANES)]
    return pl.pallas_call(
        last_kernel,
        grid=(1,),
        in_specs=[pl.BlockSpec(memory_space=pltpu.SMEM)] + [at_once(a.shape) for a in arrays],
        out_specs=tuple(at_once(shape) for shape in shapes),
        out_shape=tuple(jax.ShapeDtypeStruct(shape, jnp.float32) for shape in shapes),
        compiler_params=vmem(16),
        cost_estimate=cost(0, 10 * ROWS * 3 * D),
    )(near, *arrays)


def pairs_of(rows):
    lead = rows.shape[:-1]
    return jnp.moveaxis(rows.reshape(*lead, 3, HEADS // 2, 128), -3, -2).reshape(*lead, 3 * D)


def of_pairs(rows):
    lead = rows.shape[:-1]
    return jnp.moveaxis(rows.reshape(*lead, HEADS // 2, 3, 128), -3, -2).reshape(*lead, 3 * D)


def small_to_blocks(grad_vectors, grad_b_in, place):
    vectors = jnp.pad(
        grad_vectors.reshape(8, 4, 2, ROWS).transpose(2, 1, 0, 3),
        ((0, 0), (0, 0), (0, 8), (0, LANES - ROWS)),
    )
    biases = jnp.pad(
        grad_b_in.reshape(4, 2, 1, LANES).transpose(1, 0, 2, 3), ((0, 0), (0, 0), (0, 15), (0, 0))
    )
    vectors, biases = low(vectors), low(biases)
    return (
        jnp.where(place.c == 0, biases, vectors),
        jnp.where(place.c == 0, vectors, biases),
    )


def layer_front(tokens, context, out_weight, vector_wide):
    attn_branch = wide_dot(context, out_weight) + vector_wide[2]
    return norm_forward(wide(tokens) + attn_branch, vector_wide[3], vector_wide[4])


def layer_end(active, down, first_norm, vector_wide, valid_rows, cotangent):
    mlp_branch = wide_dot(active, down) + vector_wide[5]
    second_norm, normed_two, inverse_two = norm_forward(
        first_norm + mlp_branch, vector_wide[6], vector_wide[7]
    )
    layer_out = low(jnp.where(valid_rows[:, None], second_norm, 0.0))
    grad_out = jnp.where(valid_rows[:, None], wide(cotangent), 0.0)
    return (layer_out, *norm_backward(grad_out, normed_two, inverse_two, vector_wide[6]))


def staged_body(tokens, lengths, w_qkv, vectors, w_attn_out, w_in, b_in, w_down, cotangent):
    place = Place()
    near = place.scalars
    valid_rows, doc_ids = layout(lengths[0], tokens.shape[0])
    doc_columns = document_columns(doc_ids)

    fsdp = lax.axis_index("fsdp")
    small = lax.dynamic_update_slice(jnp.zeros((8, D), jnp.bfloat16), vectors, (0, fsdp * ROWS))
    small = jnp.concatenate([small[:, :LANES], small[:, LANES:]])
    own_b = lax.dynamic_update_slice(jnp.zeros((16, LANES), jnp.bfloat16), b_in[None], (fsdp, 0))
    own = jnp.concatenate([to_blocks(pairs_of(w_qkv), place).reshape(-1, LANES), small, own_b])
    qkv = jnp.stack([own, *turned(own)])
    qkv_y = swap_y(qkv)
    qkv_pieces = [qkv, qkv_y, swap_core(qkv), swap_core(qkv_y)]
    own = jnp.concatenate(
        [
            to_blocks(w_in, place, True).reshape(-1, LANES),
            to_blocks(w_attn_out, place, True).reshape(-1, LANES),
        ]
    )
    own = after(own, qkv)
    came = turned(own)
    own_down = to_blocks(w_down, place, down=True).reshape(-1, LANES)
    w_qkv_full, projected, vector_wide, b_full = project(
        near, after(tokens, came, own_down), qkv_pieces, HEADS // 2
    )
    rest = [jnp.stack([own, *came])]
    own_down = after(own_down, came)
    came_down = turned(own_down)
    context_lo, total_lo = attention_forward(after(projected, rest[0]), doc_columns, 0)
    rest += after([swap_y(rest[0]), swap_x(rest[0])], context_lo)
    context_hi, total_hi = attention_forward(
        after(projected, context_lo, rest[1], rest[2]), doc_columns, 3
    )
    rest.append(after(swap_x(rest[1]), context_hi))
    came_down = after(came_down, context_hi)
    down = jnp.stack([own_down, *came_down])
    down_y = swap_y(down)
    rest += [swap_core(piece) for piece in rest]
    in_full, out_full = put_together(rest_kernel, near, rest, [(D, 4 * D), (D, D)])
    context = jnp.concatenate([context_lo, context_hi], axis=1)
    first_norm, normed_one, inverse_one = layer_front(tokens, context, out_full, vector_wide)
    first_low = low(first_norm)
    active, slope = gelu_forward(first_low, in_full, b_full.reshape(-1))
    down_y = after(down_y, active)
    down_pieces = [down, down_y, swap_core(down), swap_core(down_y)]
    (down_full,) = put_together(down_kernel, near, down_pieces, [(4 * D, D)])
    layer_out, grad_two, gain_two, shift_two = layer_end(
        active, down_full, first_norm, vector_wide, valid_rows, cotangent
    )

    grad_mlp = low(grad_two)
    back_first, grad_b_in, *parts = feed_backward(
        near, grad_mlp, first_low, active, slope, down_full, in_full
    )
    down_sum = Reduction(place, *parts[:2])
    in_sum = Reduction(place, *parts[2:], split_x=True)
    grad_one, gain_one, shift_one = norm_backward(
        grad_two + back_first, normed_one, inverse_one, vector_wide[3]
    )
    grad_attn = low(grad_one)
    grad_context = low(wide_dot(grad_attn, out_full, NT))
    down_sum.send_x().send_y()
    in_sum.send_x()

    def back_of(projected, context, total, pairs, own_first, first, *others):
        return attention_backward(
            projected, doc_columns, after(grad_context, *others), context, total, pairs, own_first, first
        )

    back_a, sums_a = back_of(projected, context_lo, total_lo, 2, 0, 0, in_sum.for_x, down_sum.for_y)
    down_sum.from_y = after(down_sum.from_y, back_a)
    down_sum.send_z()
    back_b, sums_b = back_of(projected, context_lo, total_lo, 1, 2, 2, back_a, down_sum.for_z)
    in_sum.from_x = after(in_sum.from_x, back_b)
    in_sum.send_y()
    back_lo = jnp.concatenate([back_a, back_b], axis=1)
    lo_sum = Reduction(
        place, *lo_and_out_grad(near, tokens, after(back_lo, in_sum.for_y), context, grad_attn)
    )
    back_3, sums_3 = back_of(projected, context_hi, total_hi, 1, 0, 3, lo_sum.both[0], in_sum.for_y)
    lo_sum.both[1], in_sum.from_y = after((lo_sum.both[1], in_sum.from_y), back_3)
    lo_sum.send_y()
    in_sum.send_z()
    back_4, sums_4 = back_of(
        projected, context_hi, total_hi, 1, 1, 4, back_3, lo_sum.for_y, in_sum.for_z
    )
    down_sum.from_z = after(down_sum.from_z, back_4)
    down_sum.send_last_x()
    back_5, sums_5 = back_of(projected, context_hi, total_hi, 1, 2, 5, back_4, down_sum.total)
    lo_sum.from_y, down_sum.far = after((lo_sum.from_y, down_sum.far), back_5)
    grad_vectors = jnp.concatenate(
        [
            jnp.concatenate([sums_a, sums_b, sums_3, sums_4, sums_5], axis=1),
            jnp.stack(
                [
                    jnp.sum(wide(grad_attn), axis=0),
                    gain_one,
                    shift_one,
                    jnp.sum(wide(grad_mlp), axis=0),
                    gain_two,
                    shift_two,
                ]
            ),
        ]
    )
    hi_sum = Reduction(
        place,
        *hi_grad(
            near, tokens, [back_3, back_4, back_5], small_to_blocks(grad_vectors, grad_b_in, place)
        ),
    )
    lo_sum.from_y = after(lo_sum.from_y, hi_sum.both[0])
    lo_sum.send_z()
    hi_sum.both[1] = after(hi_sum.both[1], lo_sum.for_z)
    hi_sum.send_y()
    in_sum.from_z, down_sum.far = after((in_sum.from_z, down_sum.far), hi_sum.for_y)
    in_sum.send_last_x()
    down_sum.send_last_core()
    back = jnp.concatenate([back_lo, back_3, back_4, back_5], axis=1)
    grad_tokens = low(
        grad_one + wide_dot(after(back, in_sum.total, down_sum.total), w_qkv_full, NT)
    )
    hi_sum.from_y = after(hi_sum.from_y, grad_tokens)
    hi_sum.send_z()
    lo_sum.from_z, in_sum.far = after((lo_sum.from_z, in_sum.far), hi_sum.for_z)
    in_sum.send_last_core()
    lo_sum.send_last()
    hi_sum.from_z = after(hi_sum.from_z, lo_sum.total, in_sum.total)
    hi_sum.send_last()
    qkv_shard, out_shard, vector_shard, bias_shard = last_sums(near, lo_sum, hi_sum)
    return (
        layer_out,
        grad_tokens,
        qkv_shard,
        vector_shard,
        out_shard,
        from_blocks(in_sum.finish(), 8),
        bias_shard.reshape(-1),
        from_blocks(down_sum.finish(), 8, True),
    )


def plain_body(tokens, lengths, w_qkv, vectors, w_attn_out, w_in, b_in, w_down, cotangent):
    def whole(rows, axis=0):
        return lax.all_gather(rows, "fsdp", axis=axis, tiled=True)

    def own(total, axis=0):
        shard = lax.psum_scatter(total, "fsdp", scatter_dimension=axis, tiled=True)
        return wide(lax.psum(low(shard), "rep"))

    valid_rows, doc_ids = layout(lengths[0], tokens.shape[0])
    doc_columns = document_columns(doc_ids)
    qkv_full, out_full, in_full, down_full = whole(w_qkv), whole(w_attn_out), whole(w_in), whole(w_down)
    vector_wide = wide(whole(vectors, 1))
    bias = jnp.concatenate([vector_wide[0], jnp.zeros((D,), jnp.float32), vector_wide[1]])
    projected = pairs_of(low(wide_dot(tokens, qkv_full) + bias))
    context, log_total = attention_forward(projected, doc_columns, 0, HEADS // 2)
    first_norm, normed_one, inverse_one = layer_front(tokens, context, out_full, vector_wide)
    first_low = low(first_norm)
    active, slope = gelu_forward(first_low, in_full, whole(b_in))
    layer_out, grad_two, gain_two, shift_two = layer_end(
        active, down_full, first_norm, vector_wide, valid_rows, cotangent
    )
    grad_mlp = low(grad_two)
    grad_inner, grad_b_in = inner_backward(grad_mlp, down_full, slope)
    grad_first = grad_two + wide_dot(grad_inner, in_full, NT)
    grad_one, gain_one, shift_one = norm_backward(
        grad_first, normed_one, inverse_one, vector_wide[3]
    )
    grad_attn = low(grad_one)
    grad_context = low(wide_dot(grad_attn, out_full, NT))
    back, column_sums = attention_backward(
        projected, doc_columns, grad_context, context, log_total, HEADS // 2, 0, 0
    )
    back = of_pairs(back)
    edge = [
        jnp.sum(wide(grad_attn), axis=0), gain_one, shift_one, jnp.sum(wide(grad_mlp), axis=0), gain_two, shift_two
    ]
    return (
        layer_out,
        low(grad_one + wide_dot(back, qkv_full, NT)),
        own(wide_dot(tokens, back, TN)),
        own(jnp.concatenate([column_sums, jnp.stack(edge)]), 1),
        own(wide_dot(context, grad_attn, TN)),
        own(wide_dot(first_low, grad_inner, TN)),
        own(grad_b_in.reshape(-1)),
        own(wide_dot(active, grad_mlp, TN)),
    )


def solution(mesh):
    staged = mesh.shape["fsdp"] == 8 and mesh.shape["rep"] == 4
    return jax.shard_map(
        staged_body if staged else plain_body,
        mesh=mesh,
        in_specs=(
            P(("fsdp", "rep"), None),
            P(("fsdp", "rep"), None),
            P("fsdp", None),
            P(None, "fsdp"),
            P("fsdp", None),
            P("fsdp", None),
            P("fsdp"),
            P("fsdp", None),
            P(("fsdp", "rep"), None),
        ),
        out_specs=(
            P(("fsdp", "rep"), None),
            P(("fsdp", "rep"), None),
            P("fsdp", None),
            P(None, "fsdp"),
            P("fsdp", None),
            P("fsdp", None),
            P("fsdp"),
            P("fsdp", None),
        ),
        check_vma=False,
    )
```

```python
import functools
import math

import jax
import jax.numpy as jnp
from jax import lax
from jax.experimental import pallas as pl
from jax.experimental.pallas import tpu as pltpu
from jax.sharding import PartitionSpec as P

D = 768
HEADS = 12
HEAD_DIM = 64
BLOCK = 128

NORM_EPS = 1e-12
MASKED_SCORE = -1e30
SCALE_TWO = 0.125 * math.log2(math.e)
MIB = 1 << 20
CHEAP = 8

NT = (((1,), (1,)), ((), ()))
TN = (((0,), (0,)), ((), ()))


def wide_dot(left, right, dims=(((1,), (0,)), ((), ()))):
    return lax.dot_general(left, right, dims, preferred_element_type=jnp.float32)


def vmem(mib):
    return pltpu.CompilerParams(vmem_limit_bytes=mib * MIB)


def cost(flops, bytes_accessed, transcendentals=0):
    return pl.CostEstimate(
        flops=flops // CHEAP, bytes_accessed=bytes_accessed // CHEAP, transcendentals=transcendentals // CHEAP
    )


def at_once(shape):
    return pl.BlockSpec(shape, lambda i: (0,) * len(shape), pipeline_mode=pl.Buffered(1))


def layout(length_row, row_count):
    first_len = length_row[0]
    second_len = length_row[1]
    second_start = (first_len + BLOCK - 1) // BLOCK * BLOCK
    positions = jnp.arange(row_count, dtype=jnp.int32)
    in_first = positions < first_len
    in_second = (positions >= second_start) & (positions < second_start + second_len)
    doc_ids = jnp.where(in_first, 0, jnp.where(in_second, 1, 2)).astype(jnp.int32)
    return (in_first | in_second, doc_ids)


def norm_forward(hidden, gain_row, shift_row):
    centre = jnp.mean(hidden, axis=-1, keepdims=True)
    spread = jnp.mean(jnp.square(hidden - centre), axis=-1, keepdims=True)
    inverse = lax.rsqrt(spread + NORM_EPS)
    normed = (hidden - centre) * inverse
    return (normed * gain_row + shift_row, normed, inverse)


def norm_backward_rows(grad_rows, normed, inverse, gain_row):
    scaled = grad_rows * gain_row
    return inverse * (
        scaled
        - jnp.mean(scaled, axis=-1, keepdims=True)
        - normed * jnp.mean(scaled * normed, axis=-1, keepdims=True)
    )


def norm_backward(grad_rows, normed, inverse, gain_row):
    grad_in = norm_backward_rows(grad_rows, normed, inverse, gain_row)
    return (grad_in, jnp.sum(grad_rows * normed, axis=0), jnp.sum(grad_rows, axis=0))


LANES = 384
ROWS = 96
HALF = ROWS // 2


class Place:
    def __init__(self):
        fsdp, rep = lax.axis_index("fsdp"), lax.axis_index("rep")
        self.z, self.y = fsdp // 2, fsdp % 2
        self.x, self.c = rep // 2, rep % 2
        self.scalars = jnp.stack([self.z, self.y, self.x, self.c]).astype(jnp.int32)


def swap_core(rows):
    return lax.ppermute(rows, "rep", [(i, i ^ 1) for i in range(4)])


def swap_x(rows):
    return lax.ppermute(rows, "rep", [(i, i ^ 2) for i in range(4)])


def swap_y(rows):
    return lax.ppermute(rows, "fsdp", [(i, i ^ 1) for i in range(8)])


def turn_z(rows, step):
    return lax.ppermute(rows, "fsdp", [(i, (i + 2 * step) % 8) for i in range(8)])


def pick(rows, index):
    return lax.dynamic_index_in_dim(rows, index, 0, keepdims=False)


def after(rows, *others):
    return lax.optimization_barrier((rows, *others))[0]


def wide(rows):
    return rows.astype(jnp.float32)


def low(rows):
    return rows.astype(jnp.bfloat16)


def turned(own):
    return [turn_z(own, step) for step in (1, 2, 3)]


def to_blocks(shard, place, split_x=False, down=False):
    if down:
        blocks = shard.reshape(4, 2, HALF, 2, LANES).transpose(1, 3, 0, 2, 4).reshape(2, 8, HALF, LANES)
    else:
        blocks = shard.reshape(2, HALF, -1, LANES).transpose(0, 2, 1, 3)
    blocks = pick(blocks, place.c)
    if split_x:
        nb = blocks.shape[0] // 2
        blocks = lax.dynamic_slice_in_dim(blocks, place.x * nb, nb, 0)
    return blocks


def assemble(near_ref, pieces, full_ref, nb):
    z, y, c = near_ref[0], near_ref[1], near_ref[3]
    for p, piece in enumerate(pieces):
        core = 1 - c if p >> 1 else c
        for k in range(4):
            f = lax.rem(z + 4 - k, 4) * 2 + (1 - y if p & 1 else y)
            row = pl.multiple_of(f * ROWS + core * HALF, HALF)
            for j in range(nb):
                full_ref[pl.ds(row, HALF), j * LANES : (j + 1) * LANES] = piece[
                    k, j * HALF : (j + 1) * HALF
                ]


def assemble_down(near_ref, pieces, full_ref):
    z, y, c = near_ref[0], near_ref[1], near_ref[3]
    for p, piece in enumerate(pieces):
        core = 1 - c if p >> 1 else c
        for k in range(4):
            f = lax.rem(z + 4 - k, 4) * 2 + (1 - y if p & 1 else y)
            for j in range(8):
                row = pl.multiple_of(f * (4 * ROWS) + j % 4 * ROWS + core * HALF, HALF)
                col = j // 4 * LANES
                full_ref[pl.ds(row, HALF), col : col + LANES] = piece[k, j * HALF : (j + 1) * HALF]


def rest_kernel(near_ref, *refs):
    in_ref, out_ref = refs[-2:]
    z, y, x, c = near_ref[0], near_ref[1], near_ref[2], near_ref[3]
    for p, piece in enumerate(refs[:-2]):
        core = 1 - c if p >> 2 else c
        side = 1 - x if (p >> 1) & 1 else x
        for k in range(4):
            f = lax.rem(z + 4 - k, 4) * 2 + (1 - y if p & 1 else y)
            row = pl.ds(pl.multiple_of(f * ROWS + core * HALF, HALF), HALF)
            for j in range(4):
                col = pl.ds(pl.multiple_of((side * 4 + j) * LANES, LANES), LANES)
                in_ref[row, col] = piece[k, j * HALF : (j + 1) * HALF]
            col = pl.ds(pl.multiple_of(side * LANES, LANES), LANES)
            out_ref[row, col] = piece[k, 4 * HALF : 5 * HALF]


def down_kernel(near_ref, *refs):
    assemble_down(near_ref, refs[:-1], refs[-1])


def put_together(kernel, near, pieces, shapes):
    return pl.pallas_call(
        kernel,
        grid=(1,),
        out_shape=tuple(jax.ShapeDtypeStruct(shape, jnp.bfloat16) for shape in shapes),
        in_specs=[pl.BlockSpec(memory_space=pltpu.SMEM)] + [at_once(piece.shape) for piece in pieces],
        out_specs=tuple(at_once(shape) for shape in shapes),
        compiler_params=vmem(16),
        cost_estimate=cost(0, 4 * sum(math.prod(shape) for shape in shapes), 0),
    )(near, *pieces)


class Reduction:
    def __init__(self, place, mate, mine, split_x=False):
        self.place, self.split_x = place, split_x
        self.both = [mine, swap_core(mate)]

    def part(self, rows, side):
        half = rows.shape[2] // 2
        return wide(lax.dynamic_slice_in_dim(rows, side * half, half, 2))

    def send_x(self):
        place = self.place
        if self.split_x:
            self.for_x = low(sum(self.part(rows, 1 - place.x) for rows in self.both))
            self.from_x = swap_x(self.for_x)
        return self

    def half_y(self, index):
        if not self.split_x:
            return sum(wide(pick(rows, index)) for rows in self.both)
        kept = sum(pick(self.part(rows, self.place.x), index) for rows in self.both)
        return kept + wide(pick(self.from_x, index))

    def send_y(self):
        self.for_y = low(self.half_y(1 - self.place.y))
        self.from_y = swap_y(self.for_y)
        return self

    def send_z(self):
        near = self.half_y(self.place.y) + wide(self.from_y)
        self.kept = pick(near, self.place.z)
        self.for_z = [low(pick(near, (self.place.z + step) % 4)) for step in (1, 2, 3)]
        self.from_z = [turn_z(rows, step) for step, rows in zip((1, 2, 3), self.for_z, strict=True)]
        return self

    def send_last_x(self):
        self.total = low(self.kept + sum(wide(rows) for rows in self.from_z))
        self.far = swap_x(self.total)
        return self

    def send_last_core(self):
        if self.split_x:
            both = jnp.concatenate([self.total, self.far]), jnp.concatenate([self.far, self.total])
            self.total = jnp.where(self.place.x == 0, *both)
        else:
            self.total = low(wide(self.total) + wide(self.far))
        self.far = swap_core(self.total)
        return self

    def send_last(self):
        self.total = low(self.kept + sum(wide(rows) for rows in self.from_z))
        self.others = [lax.ppermute(self.total, "rep", [(i, i ^ at) for i in range(4)]) for at in (2, 1, 3)]
        return self

    def finish(self):
        both = jnp.stack([self.total, self.far]), jnp.stack([self.far, self.total])
        return wide(jnp.where(self.place.c == 0, *both))


def from_blocks(parts, nb, down=False):
    if down:
        blocks = parts.reshape(2, 2, 4, HALF, LANES)
        return blocks.transpose(2, 0, 3, 1, 4).reshape(LANES, 2 * LANES)
    return parts.reshape(2, nb, HALF, LANES).transpose(0, 2, 1, 3).reshape(ROWS, nb * LANES)


def document_columns(doc_ids):
    hot = (doc_ids[:, None] == jnp.arange(128)[None, :]) & (jnp.arange(128) < 3)[None, :]
    other = (~hot) & (jnp.arange(128) < 3)[None, :]
    return (
        jnp.where(other, MASKED_SCORE, 0.0).astype(jnp.bfloat16),
        hot.astype(jnp.bfloat16),
    )


def head_part(rows, side):
    column = lax.broadcasted_iota(jnp.int32, rows.shape, 1)
    inside = column < HEAD_DIM if side == 0 else column >= HEAD_DIM
    return jnp.where(inside, rows, jnp.zeros_like(rows))


def attend_kernel(qkv_ref, qx_ref, kx_ref, ctx_ref, lse_ref, out_scr):
    rows = qkv_ref.shape[0]
    step = rows
    keys = jnp.concatenate([qkv_ref[:, 128:256], kx_ref[...]], axis=1)
    values_t = qkv_ref[:, 256:].T
    for side in range(2):
        queries = jnp.concatenate([head_part(qkv_ref[:, :128], side), qx_ref[...]], axis=1)
        mine = slice(side * HEAD_DIM, (side + 1) * HEAD_DIM)
        for at in range(0, rows, step):
            scores = wide_dot(keys, queries[at : at + step], NT)
            top = jnp.max(scores, axis=0, keepdims=True)
            weights = jnp.exp2((scores - top) * SCALE_TWO)
            total = jnp.sum(weights, axis=0, keepdims=True)
            attended = wide_dot(values_t[mine], weights.astype(jnp.bfloat16))
            out_scr[mine, at : at + step] = attended * (1.0 / total)
            lse_ref[0, side : side + 1, at : at + step] = top * SCALE_TWO + jnp.log2(total)
    ctx_ref[...] = out_scr[...].T.astype(jnp.bfloat16)


def attention_forward(projected, doc_columns, first, pairs=3):
    rows = projected.shape[0]
    fixed = pl.BlockSpec((rows, 128), lambda h: (0, 0))
    return pl.pallas_call(
        attend_kernel,
        grid=(pairs,),
        out_shape=(
            jax.ShapeDtypeStruct((rows, pairs * 128), jnp.bfloat16),
            jax.ShapeDtypeStruct((pairs, 2, rows), jnp.float32),
        ),
        in_specs=[pl.BlockSpec((rows, 384), lambda h: (0, first + h)), fixed, fixed],
        out_specs=(
            pl.BlockSpec((rows, 128), lambda h: (0, h)),
            pl.BlockSpec((1, 2, rows), lambda h: (h, 0, 0)),
        ),
        scratch_shapes=[pltpu.VMEM((128, rows), jnp.float32)],
        compiler_params=vmem(32),
        cost_estimate=cost(16 * pairs * rows * rows * 128, 8 * rows * pairs * 128, 2 * pairs * rows * rows),
    )(projected, *doc_columns)


def attend_back_kernel(
    qkv_ref, do_ref, ctx_ref, lse_ref, qx_ref, kx_ref, out_ref, sums_ref, dq_scr
):
    rows = qkv_ref.shape[0]
    step = min(512, rows)
    grads = do_ref[...]
    product_t = (wide(grads) * wide(ctx_ref[...])).T
    keys_t = qkv_ref[:, 128:256].T
    heads = []
    for side in range(2):
        mine = slice(side * HEAD_DIM, (side + 1) * HEAD_DIM)
        q_side = head_part(qkv_ref[:, :128], side)
        heads.append((
            mine,
            q_side,
            jnp.concatenate([q_side, qx_ref[...]], axis=1),
            head_part(grads, side),
            jnp.sum(product_t[mine], axis=0, keepdims=True),
            lse_ref[0, side : side + 1, :],
        ))
    value_sum = jnp.zeros((1, 128), jnp.float32)
    for at in range(0, rows, step):
        here = slice(at, at + step)
        keys = jnp.concatenate([qkv_ref[here, 128:256], kx_ref[here]], axis=1)
        key_grad = jnp.zeros((step, 128), jnp.float32)
        value_grad = jnp.zeros((step, 128), jnp.float32)
        for mine, q_side, queries, do_side, delta, lse in heads:
            weights = jnp.exp2(wide_dot(keys, queries, NT) * SCALE_TWO - lse)
            grad_weights = wide_dot(qkv_ref[here, 256:], do_side, NT)
            grad_scores = (weights * (grad_weights - delta)).astype(jnp.bfloat16)
            value_grad += wide_dot(weights.astype(jnp.bfloat16), do_side)
            key_grad += wide_dot(grad_scores, q_side)
            query_grad = wide_dot(keys_t[mine, here], grad_scores)
            if at == 0:
                dq_scr[mine] = query_grad
            else:
                dq_scr[mine] += query_grad
        out_ref[here, 128:256] = low(key_grad * 0.125)
        value_low = low(value_grad)
        out_ref[here, 256:] = value_low
        value_sum += jnp.sum(wide(value_low), axis=0, keepdims=True)
    query_low = low(dq_scr[...].T * 0.125)
    out_ref[:, :128] = query_low
    query_sum = jnp.sum(wide(query_low), axis=0, keepdims=True)
    sums_ref[...] = jnp.concatenate([query_sum, value_sum], axis=0)


def attention_backward(projected, doc_columns, grad_context, context, log_total, pairs, own_first, first):
    rows = projected.shape[0]
    fixed = pl.BlockSpec((rows, 128), lambda h: (0, 0))
    return pl.pallas_call(
        attend_back_kernel,
        grid=(pairs,),
        out_shape=(
            jax.ShapeDtypeStruct((rows, pairs * 384), jnp.bfloat16),
            jax.ShapeDtypeStruct((2, pairs * 128), jnp.float32),
        ),
        in_specs=[
            pl.BlockSpec((rows, 384), lambda h: (0, first + h)),
            pl.BlockSpec((rows, 128), lambda h: (0, first + h)),
            pl.BlockSpec((rows, 128), lambda h: (0, own_first + h)),
            pl.BlockSpec((1, 2, rows), lambda h: (own_first + h, 0, 0)),
            fixed,
            fixed,
        ],
        out_specs=(
            pl.BlockSpec((rows, 384), lambda h: (0, h)),
            pl.BlockSpec((2, 128), lambda h: (0, h)),
        ),
        scratch_shapes=[pltpu.VMEM((128, rows), jnp.float32)],
        compiler_params=vmem(32),
        cost_estimate=cost(40 * pairs * rows * rows * 128, 18 * rows * pairs * 128, 2 * pairs * rows * rows),
    )(projected, grad_context, context, log_total, *doc_columns)


def gelu_tile(x_ref, w_ref, b_ref, act_ref, slope_ref):
    inner = wide_dot(x_ref[...], w_ref) + wide(b_ref[...])
    phi = 0.5 + 0.5 * lax.erf(inner * math.sqrt(0.5))
    bell = jnp.exp(inner * inner * -0.5) * (1.0 / math.sqrt(2.0 * math.pi))
    act_ref[...] = low(inner * phi)
    slope_ref[...] = low(phi + inner * bell)


def gelu_kernel(x_ref, w_ref, b_ref, act_ref, slope_ref):
    gelu_tile(x_ref, w_ref[...], b_ref, act_ref, slope_ref)


def gelu_forward(rows, w_in, b_in):
    count, units = rows.shape[0], w_in.shape[1]
    tile = 512
    column = pl.BlockSpec((count, tile), lambda j: (0, j))
    like = jax.ShapeDtypeStruct((count, units), jnp.bfloat16)
    return pl.pallas_call(
        gelu_kernel,
        grid=(units // tile,),
        out_shape=(like, like),
        in_specs=[
            pl.BlockSpec((count, D), lambda j: (0, 0)),
            pl.BlockSpec((D, tile), lambda j: (0, j)),
            pl.BlockSpec((1, tile), lambda j: (0, j)),
        ],
        out_specs=(column, column),
        compiler_params=vmem(32),
        cost_estimate=cost(2 * count * D * units, 4 * count * units, 2 * count * units),
    )(rows, w_in, b_in.reshape(1, -1))


def inner_grad_kernel(g_ref, w_ref, slope_ref, out_ref, sum_ref):
    grad = wide_dot(g_ref[...], w_ref[...], NT) * slope_ref[...].astype(jnp.float32)
    low = grad.astype(jnp.bfloat16)
    out_ref[...] = low
    sum_ref[...] = jnp.sum(low.astype(jnp.float32), axis=0, keepdims=True)


def inner_backward(grad_mlp, w_down, slope):
    count, units = slope.shape
    tile = 512
    column = pl.BlockSpec((count, tile), lambda j: (0, j))
    return pl.pallas_call(
        inner_grad_kernel,
        grid=(units // tile,),
        out_shape=(
            jax.ShapeDtypeStruct((count, units), jnp.bfloat16),
            jax.ShapeDtypeStruct((1, units), jnp.float32),
        ),
        in_specs=[
            pl.BlockSpec((count, D), lambda j: (0, 0)),
            pl.BlockSpec((tile, D), lambda j: (j, 0)),
            column,
        ],
        out_specs=(column, pl.BlockSpec((1, tile), lambda j: (0, j))),
        compiler_params=vmem(32),
        cost_estimate=cost(2 * count * D * units, 6 * count * units, 0),
    )(grad_mlp, w_down, slope)


def keep_halves(total, c, mate_ref, mine_ref, where_of):
    for part in range(total.shape[0] // ROWS):
        for j in range(total.shape[1] // LANES):
            first, second = (
                total[part * ROWS + at : part * ROWS + at + HALF, j * LANES : (j + 1) * LANES]
                for at in (0, HALF)
            )
            to = where_of(part, j)
            mate_ref[to] = jnp.where(c == 0, second, first)
            mine_ref[to] = jnp.where(c == 0, first, second)


def feed_back_kernel(
    near_ref, mlp_ref, low_ref, active_ref, slope_ref, down_ref, in_ref,
    first_ref, bias_ref, down_mate, down_mine, in_mate, in_mine, low_t,
):
    c = near_ref[3]
    start = pl.program_id(0) == 0

    @pl.when(start)
    def _():
        low_t[...] = low_ref[...].T

    grad_inner = low(wide_dot(mlp_ref[...], down_ref[...], NT) * wide(slope_ref[...]))
    bias_ref[...] = jnp.sum(wide(grad_inner), axis=0, keepdims=True)

    def of_in(part, j):
        return (part % 2, part // 2, slice(j * HALF, (j + 1) * HALF))

    def of_down(part, j):
        return (part // 4, 0, slice((j * 4 + part % 4) * HALF, (j * 4 + part % 4 + 1) * HALF))

    keep_halves(low(wide_dot(low_t[...], grad_inner)), c, in_mate, in_mine, of_in)
    keep_halves(low(wide_dot(active_ref[...], mlp_ref[...], TN)), c, down_mate, down_mine, of_down)
    back = wide_dot(grad_inner, in_ref[...], NT)

    @pl.when(start)
    def _():
        first_ref[...] = back

    @pl.when(jnp.logical_not(start))
    def _():
        first_ref[...] += back


def feed_backward(near, grad_mlp, first_low, active, slope, down_full, in_full):
    count, units = active.shape
    tile = 2 * LANES
    rows = 8 * HALF
    fixed = pl.BlockSpec((count, D), lambda u: (0, 0), pipeline_mode=pl.Buffered(1))
    column = pl.BlockSpec((count, tile), lambda u: (0, u))
    like = jax.ShapeDtypeStruct((2, 4, rows, LANES), jnp.bfloat16)
    down_out = pl.BlockSpec((2, 1, rows, LANES), lambda u: (0, u, 0, 0))
    in_out = pl.BlockSpec((2, 4, 2 * HALF, LANES), lambda u: (0, 0, u, 0))
    return pl.pallas_call(
        feed_back_kernel,
        grid=(units // tile,),
        in_specs=[
            pl.BlockSpec(memory_space=pltpu.SMEM),
            fixed,
            fixed,
            column,
            column,
            pl.BlockSpec((tile, D), lambda u: (u, 0)),
            pl.BlockSpec((D, tile), lambda u: (0, u)),
        ],
        out_specs=(
            pl.BlockSpec((count, D), lambda u: (0, 0)),
            pl.BlockSpec((1, tile), lambda u: (0, u)),
            down_out, down_out, in_out, in_out,
        ),
        out_shape=(
            jax.ShapeDtypeStruct((count, D), jnp.float32),
            jax.ShapeDtypeStruct((1, units), jnp.float32),
            like, like, like, like,
        ),
        scratch_shapes=[pltpu.VMEM((D, count), jnp.bfloat16)],
        compiler_params=vmem(48),
        cost_estimate=cost(8 * count * D * units, 8 * count * units),
    )(near, grad_mlp, first_low, active, slope, down_full, in_full)


def qkv_grad_kernel(many, near_ref, *refs):
    left_ref, rights, edges = refs[0], refs[1 : 1 + many], refs[1 + many : -2]
    mate_ref, mine_ref = refs[-2:]
    c = near_ref[3]
    right = jnp.concatenate([ref[...] for ref in rights], axis=1)
    blocks = right.shape[1] // LANES

    def where_of(part, j):
        return (part % 2, part // 2, slice(j * HALF, (j + 1) * HALF))

    keep_halves(low(wide_dot(left_ref[...], right, TN)), c, mate_ref, mine_ref, where_of)
    for ref, edge in zip((mate_ref, mine_ref), edges, strict=True):
        ref[:, :, blocks * HALF :] = edge[...]


def out_grad_kernel(near_ref, left_ref, right_ref, edge_left, edge_right, mate_ref, mine_ref):
    c = near_ref[3]

    def where_of(part, j):
        return (part % 2, part // 2, slice(j * HALF, (j + 1) * HALF))

    keep_halves(low(wide_dot(left_ref[...], right_ref[...], TN)), c, mate_ref, mine_ref, where_of)
    blocks = right_ref.shape[1] // LANES

    def edge_of(part, j):
        return (part % 2, part // 2, slice((blocks + j) * HALF, (blocks + j + 1) * HALF))

    keep_halves(low(wide_dot(edge_left[...], edge_right[...], TN)), c, mate_ref, mine_ref, edge_of)


def whole_grad(kernel, near, arrays, rows, flops, mib=32):
    like = jax.ShapeDtypeStruct((2, 4, rows, LANES), jnp.bfloat16)
    return pl.pallas_call(
        kernel,
        grid=(1,),
        in_specs=[pl.BlockSpec(memory_space=pltpu.SMEM)] + [at_once(a.shape) for a in arrays],
        out_specs=(at_once(like.shape),) * 2,
        out_shape=(like, like),
        compiler_params=vmem(mib),
        cost_estimate=cost(flops, sum(2 * a.size for a in arrays), 0),
    )(near, *arrays)


def lo_and_out_grad(near, left, right, out_left, out_right):
    rows = (right.shape[1] + out_right.shape[1]) // LANES * HALF
    flops = 2 * left.shape[0] * D * (right.shape[1] + out_right.shape[1])
    return whole_grad(out_grad_kernel, near, [left, right, out_left, out_right], rows, flops)


def hi_grad(near, left, rights, edges):
    width = sum(right.shape[1] for right in rights)
    rows = width // LANES * HALF + edges[0].shape[2]
    kernel = functools.partial(qkv_grad_kernel, len(rights))
    return whole_grad(kernel, near, [left, *rights, *edges], rows, 2 * left.shape[0] * D * width, 60)


def project_kernel(nb, near_ref, tokens_ref, *refs):
    pieces = refs[:4]
    full_ref, out_ref, vec_ref, b_ref = refs[4:]
    small = sum(
        wide(piece[k, nb * HALF : nb * HALF + 24]) for piece in pieces[:2] for k in range(4)
    )
    vec_ref[:, :LANES] = small[:8]
    vec_ref[:, LANES:] = small[8:16]
    for f in range(8):
        b_ref[:, f * LANES : (f + 1) * LANES] = small[16 + f : 17 + f]
    assemble(near_ref, pieces, full_ref, nb)
    for j in range(nb):
        here = slice(j * LANES, (j + 1) * LANES)
        pair = slice(j * 128, (j + 1) * 128)
        bias = jnp.concatenate(
            [vec_ref[0:1, pair], jnp.zeros((1, 128), jnp.float32), vec_ref[1:2, pair]], axis=1
        )
        out_ref[:, here] = low(wide_dot(tokens_ref[...], full_ref[:, here]) + bias)


def project(near, tokens, pieces, nb):
    count = tokens.shape[0]
    out_shape = (
        jax.ShapeDtypeStruct((D, nb * LANES), jnp.bfloat16),
        jax.ShapeDtypeStruct((count, nb * LANES), jnp.bfloat16),
        jax.ShapeDtypeStruct((8, D), jnp.float32),
        jax.ShapeDtypeStruct((1, 4 * D), jnp.float32),
    )
    return pl.pallas_call(
        functools.partial(project_kernel, nb),
        grid=(1,),
        out_shape=out_shape,
        in_specs=[pl.BlockSpec(memory_space=pltpu.SMEM)]
        + [at_once(a.shape) for a in (tokens, *pieces)],
        out_specs=tuple(at_once(like.shape) for like in out_shape),
        compiler_params=vmem(32),
        cost_estimate=cost(2 * count * D * nb * LANES, 6 * count * D),
    )(near, tokens, *pieces)


def last_kernel(near_ref, *refs):
    qkv_ref, out_ref, vec_ref, b_ref = refs[-4:]
    c = near_ref[3]
    first_pair = 0
    for total, x, core, both in (refs[:4], refs[4:8]):
        mine, theirs = wide(total[...]) + wide(x[...]), wide(core[...]) + wide(both[...])
        parts = jnp.where(c == 0, mine, theirs), jnp.where(c == 0, theirs, mine)
        for at, part in enumerate(parts):
            rows = slice(at * HALF, (at + 1) * HALF)
            for j in range(3):
                for kind in range(3):
                    col = kind * D + (first_pair + j) * 128
                    qkv_ref[rows, col : col + 128] = part[
                        j * HALF : (j + 1) * HALF, kind * 128 : (kind + 1) * 128
                    ]
            if first_pair == 0:
                for j in range(2):
                    out_ref[rows, j * LANES : (j + 1) * LANES] = part[(3 + j) * HALF : (4 + j) * HALF]
            elif at == 0:
                vec_ref[...] = part[3 * HALF : 3 * HALF + 8, :ROWS]
            else:
                b_ref[...] = part[3 * HALF : 3 * HALF + 1]
        first_pair += 3


def last_sums(near, lo_sum, hi_sum):
    arrays = [lo_sum.total, *lo_sum.others, hi_sum.total, *hi_sum.others]
    shapes = [(ROWS, 3 * D), (ROWS, D), (8, ROWS), (1, LANES)]
    return pl.pallas_call(
        last_kernel,
        grid=(1,),
        in_specs=[pl.BlockSpec(memory_space=pltpu.SMEM)] + [at_once(a.shape) for a in arrays],
        out_specs=tuple(at_once(shape) for shape in shapes),
        out_shape=tuple(jax.ShapeDtypeStruct(shape, jnp.float32) for shape in shapes),
        compiler_params=vmem(16),
        cost_estimate=cost(0, 10 * ROWS * 3 * D),
    )(near, *arrays)


def pairs_of(rows):
    lead = rows.shape[:-1]
    return jnp.moveaxis(rows.reshape(*lead, 3, HEADS // 2, 128), -3, -2).reshape(*lead, 3 * D)


def of_pairs(rows):
    lead = rows.shape[:-1]
    return jnp.moveaxis(rows.reshape(*lead, HEADS // 2, 3, 128), -3, -2).reshape(*lead, 3 * D)


def small_to_blocks(grad_vectors, grad_b_in, place):
    vectors = jnp.pad(
        grad_vectors.reshape(8, 4, 2, ROWS).transpose(2, 1, 0, 3),
        ((0, 0), (0, 0), (0, 8), (0, LANES - ROWS)),
    )
    biases = jnp.pad(
        grad_b_in.reshape(4, 2, 1, LANES).transpose(1, 0, 2, 3), ((0, 0), (0, 0), (0, 15), (0, 0))
    )
    vectors, biases = low(vectors), low(biases)
    return (
        jnp.where(place.c == 0, biases, vectors),
        jnp.where(place.c == 0, vectors, biases),
    )


def layer_front(tokens, context, out_weight, vector_wide):
    attn_branch = wide_dot(context, out_weight) + vector_wide[2]
    return norm_forward(wide(tokens) + attn_branch, vector_wide[3], vector_wide[4])


def layer_end(active, down, first_norm, vector_wide, valid_rows, cotangent):
    mlp_branch = wide_dot(active, down) + vector_wide[5]
    second_norm, normed_two, inverse_two = norm_forward(
        first_norm + mlp_branch, vector_wide[6], vector_wide[7]
    )
    layer_out = low(jnp.where(valid_rows[:, None], second_norm, 0.0))
    grad_out = jnp.where(valid_rows[:, None], wide(cotangent), 0.0)
    return (layer_out, *norm_backward(grad_out, normed_two, inverse_two, vector_wide[6]))


def staged_body(tokens, lengths, w_qkv, vectors, w_attn_out, w_in, b_in, w_down, cotangent):
    place = Place()
    near = place.scalars
    valid_rows, doc_ids = layout(lengths[0], tokens.shape[0])
    doc_columns = document_columns(doc_ids)

    fsdp = lax.axis_index("fsdp")
    small = lax.dynamic_update_slice(jnp.zeros((8, D), jnp.bfloat16), vectors, (0, fsdp * ROWS))
    small = jnp.concatenate([small[:, :LANES], small[:, LANES:]])
    own_b = lax.dynamic_update_slice(jnp.zeros((16, LANES), jnp.bfloat16), b_in[None], (fsdp, 0))
    own = jnp.concatenate([to_blocks(pairs_of(w_qkv), place).reshape(-1, LANES), small, own_b])
    qkv = jnp.stack([own, *turned(own)])
    qkv_y = swap_y(qkv)
    qkv_pieces = [qkv, qkv_y, swap_core(qkv), swap_core(qkv_y)]
    own = jnp.concatenate(
        [
            to_blocks(w_in, place, True).reshape(-1, LANES),
            to_blocks(w_attn_out, place, True).reshape(-1, LANES),
        ]
    )
    own = after(own, qkv)
    came = turned(own)
    own_down = to_blocks(w_down, place, down=True).reshape(-1, LANES)
    w_qkv_full, projected, vector_wide, b_full = project(
        near, after(tokens, came, own_down), qkv_pieces, HEADS // 2
    )
    rest = [jnp.stack([own, *came])]
    own_down = after(own_down, came)
    came_down = turned(own_down)
    context_lo, total_lo = attention_forward(after(projected, rest[0]), doc_columns, 0)
    rest += after([swap_y(rest[0]), swap_x(rest[0])], context_lo)
    context_hi, total_hi = attention_forward(
        after(projected, context_lo, rest[1], rest[2]), doc_columns, 3
    )
    rest.append(after(swap_x(rest[1]), context_hi))
    came_down = after(came_down, context_hi)
    down = jnp.stack([own_down, *came_down])
    down_y = swap_y(down)
    rest += [swap_core(piece) for piece in rest]
    in_full, out_full = put_together(rest_kernel, near, rest, [(D, 4 * D), (D, D)])
    context = jnp.concatenate([context_lo, context_hi], axis=1)
    first_norm, normed_one, inverse_one = layer_front(tokens, context, out_full, vector_wide)
    first_low = low(first_norm)
    active, slope = gelu_forward(first_low, in_full, b_full.reshape(-1))
    down_y = after(down_y, active)
    down_pieces = [down, down_y, swap_core(down), swap_core(down_y)]
    (down_full,) = put_together(down_kernel, near, down_pieces, [(4 * D, D)])
    layer_out, grad_two, gain_two, shift_two = layer_end(
        active, down_full, first_norm, vector_wide, valid_rows, cotangent
    )

    grad_mlp = low(grad_two)
    back_first, grad_b_in, *parts = feed_backward(
        near, grad_mlp, first_low, active, slope, down_full, in_full
    )
    down_sum = Reduction(place, *parts[:2])
    in_sum = Reduction(place, *parts[2:], split_x=True)
    grad_one, gain_one, shift_one = norm_backward(
        grad_two + back_first, normed_one, inverse_one, vector_wide[3]
    )
    grad_attn = low(grad_one)
    grad_context = low(wide_dot(grad_attn, out_full, NT))
    down_sum.send_x().send_y()
    in_sum.send_x()

    def back_of(projected, context, total, pairs, own_first, first, *others):
        return attention_backward(
            projected, doc_columns, after(grad_context, *others), context, total, pairs, own_first, first
        )

    back_a, sums_a = back_of(projected, context_lo, total_lo, 2, 0, 0, in_sum.for_x, down_sum.for_y)
    down_sum.from_y = after(down_sum.from_y, back_a)
    down_sum.send_z()
    back_b, sums_b = back_of(projected, context_lo, total_lo, 1, 2, 2, back_a, down_sum.for_z)
    in_sum.from_x = after(in_sum.from_x, back_b)
    in_sum.send_y()
    back_lo = jnp.concatenate([back_a, back_b], axis=1)
    lo_sum = Reduction(
        place, *lo_and_out_grad(near, tokens, after(back_lo, in_sum.for_y), context, grad_attn)
    )
    back_3, sums_3 = back_of(projected, context_hi, total_hi, 1, 0, 3, lo_sum.both[0], in_sum.for_y)
    lo_sum.both[1], in_sum.from_y = after((lo_sum.both[1], in_sum.from_y), back_3)
    lo_sum.send_y()
    in_sum.send_z()
    back_4, sums_4 = back_of(
        projected, context_hi, total_hi, 1, 1, 4, back_3, lo_sum.for_y, in_sum.for_z
    )
    down_sum.from_z = after(down_sum.from_z, back_4)
    down_sum.send_last_x()
    back_5, sums_5 = back_of(projected, context_hi, total_hi, 1, 2, 5, back_4, down_sum.total)
    lo_sum.from_y, down_sum.far = after((lo_sum.from_y, down_sum.far), back_5)
    grad_vectors = jnp.concatenate(
        [
            jnp.concatenate([sums_a, sums_b, sums_3, sums_4, sums_5], axis=1),
            jnp.stack(
                [
                    jnp.sum(wide(grad_attn), axis=0),
                    gain_one,
                    shift_one,
                    jnp.sum(wide(grad_mlp), axis=0),
                    gain_two,
                    shift_two,
                ]
            ),
        ]
    )
    hi_sum = Reduction(
        place,
        *hi_grad(
            near, tokens, [back_3, back_4, back_5], small_to_blocks(grad_vectors, grad_b_in, place)
        ),
    )
    lo_sum.from_y = after(lo_sum.from_y, hi_sum.both[0])
    lo_sum.send_z()
    hi_sum.both[1] = after(hi_sum.both[1], lo_sum.for_z)
    hi_sum.send_y()
    in_sum.from_z, down_sum.far = after((in_sum.from_z, down_sum.far), hi_sum.for_y)
    in_sum.send_last_x()
    down_sum.send_last_core()
    back = jnp.concatenate([back_lo, back_3, back_4, back_5], axis=1)
    grad_tokens = low(
        grad_one + wide_dot(after(back, in_sum.total, down_sum.total), w_qkv_full, NT)
    )
    hi_sum.from_y = after(hi_sum.from_y, grad_tokens)
    hi_sum.send_z()
    lo_sum.from_z, in_sum.far = after((lo_sum.from_z, in_sum.far), hi_sum.for_z)
    in_sum.send_last_core()
    lo_sum.send_last()
    hi_sum.from_z = after(hi_sum.from_z, lo_sum.total, in_sum.total)
    hi_sum.send_last()
    qkv_shard, out_shard, vector_shard, bias_shard = last_sums(near, lo_sum, hi_sum)
    return (
        layer_out,
        grad_tokens,
        qkv_shard,
        vector_shard,
        out_shard,
        from_blocks(in_sum.finish(), 8),
        bias_shard.reshape(-1),
        from_blocks(down_sum.finish(), 8, True),
    )


def plain_body(tokens, lengths, w_qkv, vectors, w_attn_out, w_in, b_in, w_down, cotangent):
    def whole(rows, axis=0):
        return lax.all_gather(rows, "fsdp", axis=axis, tiled=True)

    def own(total, axis=0):
        shard = lax.psum_scatter(total, "fsdp", scatter_dimension=axis, tiled=True)
        return wide(lax.psum(low(shard), "rep"))

    valid_rows, doc_ids = layout(lengths[0], tokens.shape[0])
    doc_columns = document_columns(doc_ids)
    qkv_full, out_full, in_full, down_full = whole(w_qkv), whole(w_attn_out), whole(w_in), whole(w_down)
    vector_wide = wide(whole(vectors, 1))
    bias = jnp.concatenate([vector_wide[0], jnp.zeros((D,), jnp.float32), vector_wide[1]])
    projected = pairs_of(low(wide_dot(tokens, qkv_full) + bias))
    context, log_total = attention_forward(projected, doc_columns, 0, HEADS // 2)
    first_norm, normed_one, inverse_one = layer_front(tokens, context, out_full, vector_wide)
    first_low = low(first_norm)
    active, slope = gelu_forward(first_low, in_full, whole(b_in))
    layer_out, grad_two, gain_two, shift_two = layer_end(
        active, down_full, first_norm, vector_wide, valid_rows, cotangent
    )
    grad_mlp = low(grad_two)
    grad_inner, grad_b_in = inner_backward(grad_mlp, down_full, slope)
    grad_first = grad_two + wide_dot(grad_inner, in_full, NT)
    grad_one, gain_one, shift_one = norm_backward(
        grad_first, normed_one, inverse_one, vector_wide[3]
    )
    grad_attn = low(grad_one)
    grad_context = low(wide_dot(grad_attn, out_full, NT))
    back, column_sums = attention_backward(
        projected, doc_columns, grad_context, context, log_total, HEADS // 2, 0, 0
    )
    back = of_pairs(back)
    edge = [
        jnp.sum(wide(grad_attn), axis=0), gain_one, shift_one, jnp.sum(wide(grad_mlp), axis=0), gain_two, shift_two
    ]
    return (
        layer_out,
        low(grad_one + wide_dot(back, qkv_full, NT)),
        own(wide_dot(tokens, back, TN)),
        own(jnp.concatenate([column_sums, jnp.stack(edge)]), 1),
        own(wide_dot(context, grad_attn, TN)),
        own(wide_dot(first_low, grad_inner, TN)),
        own(grad_b_in.reshape(-1)),
        own(wide_dot(active, grad_mlp, TN)),
    )


def solution(mesh):
    staged = mesh.shape["fsdp"] == 8 and mesh.shape["rep"] == 4
    return jax.shard_map(
        staged_body if staged else plain_body,
        mesh=mesh,
        in_specs=(
            P(("fsdp", "rep"), None),
            P(("fsdp", "rep"), None),
            P("fsdp", None),
            P(None, "fsdp"),
            P("fsdp", None),
            P("fsdp", None),
            P("fsdp"),
            P("fsdp", None),
            P(("fsdp", "rep"), None),
        ),
        out_specs=(
            P(("fsdp", "rep"), None),
            P(("fsdp", "rep"), None),
            P("fsdp", None),
            P(None, "fsdp"),
            P("fsdp", None),
            P("fsdp", None),
            P("fsdp"),
            P("fsdp", None),
        ),
        check_vma=False,
    )
```
